512 devices in a mesh: row: 16 (over z), col: 16 (over x, y), grp: 2 (over core).
Axes of the slice: x: 4, y: 4, z: 16, core: 2. Of those that a mesh axis runs over, the one named last changes fastest.
Arguments:
- grad: bfloat16 [2, 8192, 4096], P('grp', 'row', 'col'), may hold values from -40000 to 40000
- exp_avg: bfloat16 [2, 8192, 4096], P('grp', 'row', 'col'), may hold values from -0.29882812 to 0.29882812
- exp_avg_sq: bfloat16 [2, 8192, 4096], P('grp', 'row', 'col'), may hold values from 0.019897461 to 0.19921875
- left_basis: bfloat16 [2, 8192, 512], P('grp', 'row'), may hold values from -5 to 5
- right_basis: bfloat16 [2, 4096, 256], P('grp', 'col'), may hold values from -5 to 5
- left_stats: float32 [2, 8192, 512], P('grp', 'row', 'col'), may hold values from -0.1 to 0.3, as said below
- right_statistics_blocks: float32 [2, 4096, 256], P('grp', 'col', 'row'), may hold values from -0.1 to 0.3, as said below
Outputs:
- update: bfloat16 [2, 8192, 4096], P('grp', 'row', 'col')
- new_exp_avg: bfloat16 [2, 8192, 4096], P('grp', 'row', 'col')
- new_exp_avg_sq: bfloat16 [2, 8192, 4096], P('grp', 'row', 'col')
- new_left_basis: bfloat16 [2, 8192, 512], P('grp', 'row')
- new_right_basis: bfloat16 [2, 4096, 256], P('grp', 'col')
- new_left_stats: float32 [2, 8192, 512], P('grp', 'row', 'col')
- new_right_stats: float32 [2, 4096, 256], P('grp', 'col', 'row')
The draws below stay inside these ranges and needn't reach their ends.
Inputs may be any that keep to these rules, and one draw needn't show every extreme that they name: `left_stats`: each of its 512 x 512 blocks is symmetric. `right_statistics_blocks`: each of its 256 x 256 blocks is symmetric.
All inputs are finite; a program needn't handle non-finite values.
Results may differ from the reference program's by a relative error of at most 0.006.
Values may be sent and summed in bfloat16 or wider, within the bound.
A program may use at most 64 MiB of HBM per device.

```python
import math
import jax
import jax.numpy as jnp
from jax import lax

LEFT_BLOCK = 512
RIGHT_BLOCK = 256
NS_STEPS = 3
ROWS = 8192
COLS = 4096
MATS = 2


def assemble_stats(base_draw, diag_key, count, blocks, width):
    diag_values = jnp.exp(jax.random.uniform(diag_key, (count, blocks, width), jnp.float32, math.log(0.02), math.log(0.2)))
    identity = jnp.eye(width, dtype=jnp.float32)
    paired = 0.01 * (base_draw + jnp.swapaxes(base_draw, -1, -2))
    return (paired + identity * diag_values[..., None]).reshape(count, blocks * width, width)


def draw_grad(key, part):
    key = jax.random.fold_in(key, 3)
    subkeys = jax.random.split(key, 3)
    full_shape = (MATS, ROWS, COLS)
    row_ramp = 1.0 + 2.0 * jnp.arange(ROWS, dtype=jnp.float32) / (ROWS - 1)
    col_ramp = 1.0 + 2.0 * jnp.arange(COLS, dtype=jnp.float32) / (COLS - 1)
    row_factor = jnp.power(10.0, jax.random.uniform(subkeys[1], (MATS, ROWS, 1), jnp.float32)) * row_ramp[None, :, None]
    col_factor = jnp.power(10.0, jax.random.uniform(subkeys[2], (MATS, 1, COLS), jnp.float32)) * col_ramp[None, None, :]
    mixed_draw = jax.random.truncated_normal(subkeys[0], -4.0, 4.0, full_shape, jnp.float32)
    return (mixed_draw * row_factor * col_factor).astype(jnp.bfloat16)


def draw_left_stats(key, part):
    key = jax.random.fold_in(key, 7)
    base_key, diag_key = jax.random.split(key)
    blocks = ROWS // LEFT_BLOCK
    block_shape = (MATS, blocks, LEFT_BLOCK, LEFT_BLOCK)
    base_draw = jax.random.truncated_normal(base_key, -4.0, 4.0, block_shape, jnp.float32)
    return assemble_stats(base_draw, diag_key, MATS, blocks, LEFT_BLOCK)


def draw_right_statistics_blocks(key, part):
    key = jax.random.fold_in(key, 13)
    base_key, diag_key = jax.random.split(key)
    blocks = COLS // RIGHT_BLOCK
    block_shape = (MATS, blocks, RIGHT_BLOCK, RIGHT_BLOCK)
    base_draw = jax.random.truncated_normal(base_key, -4.0, 4.0, block_shape, jnp.float32)
    return assemble_stats(base_draw, diag_key, MATS, blocks, RIGHT_BLOCK)


def levels(stream_key, shape, cuts, least, top_value):
    def one(position, blocks):
        heights = jax.random.uniform(jax.random.fold_in(jax.random.fold_in(stream_key, 6), position), (blocks,), jnp.float32, least / len(cuts), top_value / len(cuts))
        return jnp.repeat(jnp.exp(heights), shape[position] // blocks).reshape((-1,) + (1,) * (len(shape) - position - 1))

    gain = one(*cuts[0])
    for cut in cuts[1:]:
        gain = gain * one(*cut)
    return gain


def scatter_about(stream_key, shape, scale, limit, cuts=(), held_as=jnp.bfloat16):
    array = jax.random.normal(stream_key, shape, jnp.float32) * scale
    if len(cuts) > 0:
        array = levels(stream_key, shape, cuts, -0.22, 0.18) * array
    return jnp.clip(array, min=-limit, max=limit).astype(held_as)


def setup_inputs(seed: int = 0) -> dict:
    keys = jax.random.split(jax.random.key(seed), 8)
    return {
        "grad": draw_grad(jax.random.fold_in(keys[7], 71), 0),
        "exp_avg": scatter_about(keys[1], (MATS, ROWS, COLS), 0.05, 0.29882812, ((0, 2), (1, 16), (2, 16))),
        "exp_avg_sq": jnp.clip(jnp.exp(math.log(0.19921875) - 2.3038113 * jax.random.uniform(keys[2], (MATS, ROWS, COLS), jnp.float32) ** levels(keys[2], (MATS, ROWS, COLS), ((0, 2), (1, 16), (2, 16)), -0.2, 0.2)), 0.019897461, 0.19921875).astype(jnp.bfloat16),
        "left_basis": scatter_about(keys[3], (MATS, ROWS, LEFT_BLOCK), 1.0, 5.0, ((0, 2), (1, 16))),
        "right_basis": scatter_about(keys[4], (MATS, COLS, RIGHT_BLOCK), 1.0, 5.0, ((0, 2), (1, 16))),
        "left_stats": draw_left_stats(jax.random.fold_in(keys[7], 71), 0),
        "right_statistics_blocks": draw_right_statistics_blocks(jax.random.fold_in(keys[7], 71), 0),
    }


NS_COEFFS = (3.4445, -4.775, 2.0315)
BETA_FIRST = 0.9
BETA_SECOND = 0.99
STATISTICS_DECAY = 0.95
ADAM_EPS = 1e-08
NORM_EPS = 1e-06
MATMUL_PRECISION = lax.Precision.HIGHEST

def round_bfloat(value):
    return lax.optimization_barrier(value.astype(jnp.bfloat16)).astype(jnp.float32)

def gram_of(current):
    return lax.dot_general(current, current, (((0,), (0,)), ((), ())), precision=MATMUL_PRECISION)

def quintic(current, gram_sum):
    inner_poly = NS_COEFFS[1] * gram_sum + NS_COEFFS[2] * jnp.dot(gram_sum, gram_sum, precision=MATMUL_PRECISION)
    return NS_COEFFS[0] * current + jnp.dot(current, inner_poly, precision=MATMUL_PRECISION)

def orthogonalize(block_panel):
    current = block_panel * lax.rsqrt(jnp.sum(block_panel * block_panel) + NORM_EPS)
    for sweep_index in range(NS_STEPS):
        current = quintic(current, gram_of(current))
    return current

def reference(grad, exp_avg, exp_avg_sq, left_basis, right_basis, left_stats, right_statistics_blocks):
    row_blocks = ROWS // LEFT_BLOCK
    col_blocks = COLS // RIGHT_BLOCK
    tile_shape = (MATS, row_blocks, LEFT_BLOCK, col_blocks, RIGHT_BLOCK)
    gradient_broad = grad.astype(jnp.float32).reshape(tile_shape)
    left_broad_matrix = left_basis.astype(jnp.float32).reshape(MATS, row_blocks, LEFT_BLOCK, LEFT_BLOCK)
    right_wide = right_basis.astype(jnp.float32).reshape(MATS, col_blocks, RIGHT_BLOCK, RIGHT_BLOCK)
    total_sq = jnp.sum(gradient_broad * gradient_broad)
    max_norm = math.sqrt(MATS * ROWS * COLS)
    clip_factor = jnp.minimum(1.0, max_norm * lax.rsqrt(total_sq + NORM_EPS))
    inv_scale = 1.0 / math.sqrt(LEFT_BLOCK * RIGHT_BLOCK)
    half_turn = round_bfloat(jnp.einsum('mira,mirjb->miajb', left_broad_matrix, gradient_broad))
    raw_turn = jnp.einsum('miajb,mjbc->miajc', half_turn, right_wide)
    rotated = raw_turn * (clip_factor * inv_scale)
    first = BETA_FIRST * exp_avg.astype(jnp.float32).reshape(tile_shape) + (1.0 - BETA_FIRST) * rotated
    second = BETA_SECOND * exp_avg_sq.astype(jnp.float32).reshape(tile_shape) + (1.0 - BETA_SECOND) * rotated * rotated
    direction = round_bfloat(first / (jnp.sqrt(second) + ADAM_EPS))
    back_half = round_bfloat(jnp.einsum('mira,miajc->mirjc', left_broad_matrix, direction))
    update = jnp.einsum('mirjc,mjbc->mirjb', back_half, right_wide) * inv_scale
    left_statistics_total = jnp.einsum('hxlfe,hxkfe->hxlk', gradient_broad, gradient_broad)
    right_sum = jnp.einsum('mirjb,mirjc->mjbc', gradient_broad, gradient_broad)
    clip_sq = clip_factor * clip_factor
    left_old = left_stats.reshape(MATS, row_blocks, LEFT_BLOCK, LEFT_BLOCK)
    right_old = right_statistics_blocks.reshape(MATS, col_blocks, RIGHT_BLOCK, RIGHT_BLOCK)
    fresh_left_statistics = STATISTICS_DECAY * left_old + (1.0 - STATISTICS_DECAY) * (clip_sq / COLS) * left_statistics_total
    right_new = STATISTICS_DECAY * right_old + (1.0 - STATISTICS_DECAY) * (clip_sq / ROWS) * right_sum
    left_gradient_product = jnp.einsum('ptxh,pthd->ptxd', fresh_left_statistics, left_broad_matrix, precision=MATMUL_PRECISION)
    right_product = jnp.einsum('mjbc,mjca->mjba', right_new, right_wide, precision=MATMUL_PRECISION)
    left_orth = jax.vmap(jax.vmap(orthogonalize))(left_gradient_product)
    right_orth = jax.vmap(jax.vmap(orthogonalize))(right_product)
    new_left_basis = (left_orth * math.sqrt(LEFT_BLOCK)).astype(jnp.bfloat16).reshape(MATS, ROWS, LEFT_BLOCK)
    new_right_basis = (right_orth * math.sqrt(RIGHT_BLOCK)).astype(jnp.bfloat16).reshape(MATS, COLS, RIGHT_BLOCK)
    full_shape = (MATS, ROWS, COLS)
    return (update.astype(jnp.bfloat16).reshape(full_shape), first.astype(jnp.bfloat16).reshape(full_shape), second.astype(jnp.bfloat16).reshape(full_shape), new_left_basis, new_right_basis, fresh_left_statistics.reshape(MATS, ROWS, LEFT_BLOCK), right_new.reshape(MATS, COLS, RIGHT_BLOCK))
```

```python
import functools
import math

import jax
import jax.numpy as jnp
from jax import lax
from jax.experimental import pallas as pl
from jax.experimental.pallas import tpu as pltpu
from jax.sharding import PartitionSpec as P

NS_STEPS = 3
NS_COEFFS = (3.4445, -4.775, 2.0315)
BETA_FIRST = 0.9
BETA_SECOND = 0.99
STATISTICS_DECAY = 0.95
ADAM_EPS = 1e-08
NORM_EPS = 1e-06
F32 = jnp.float32
BF16 = jnp.bfloat16
MESH = pl.DeviceIdType.MESH
NN = (((1,), (0,)), ((), ()))
NT = (((1,), (1,)), ((), ()))
TN = (((0,), (0,)), ((), ()))


def mm(a, b, dims=NN):
    return lax.dot_general(a, b, dims, preferred_element_type=F32)


def halves(x):
    hi = x.astype(BF16)
    return hi, (x - hi.astype(F32)).astype(BF16)


def mm3(a, b, dims=NN):
    return mm(a[0], b[0], dims) + (mm(a[0], b[1], dims) + mm(a[1], b[0], dims))


def exchange_kernel(
    sizes,
    g_ref, m_ref, v_ref, ql_ref, qr_ref, lold_ref, rold_ref,
    upd_ref, first_ref, second_ref, lfull_out, rfull_out, lnew_ref, rnew_ref,
    lpart, rpart, lin, rin, lfull, rfull, sq_out, sq_plane, sq_mid, sq_line, rot, direction,
    sq_sems, l_sems, r_sems, out_sems,
):
    n_row, n_col, n_grp, max_norm = sizes
    left, right = g_ref.shape
    bl, br = left // n_col, right // n_row
    row, col, grp = lax.axis_index("row"), lax.axis_index("col"), lax.axis_index("grp")
    n_plane = n_col * n_grp
    place = col * n_grp + grp

    def plane_peer(q):
        other = lax.rem(place + q, n_plane)
        return {"col": other // n_grp, "grp": lax.rem(other, n_grp)}

    barrier = pltpu.get_barrier_semaphore()

    @pl.loop(1, n_plane)
    def _(q):
        pl.semaphore_signal(barrier, inc=1, device_id=plane_peer(q), device_id_type=MESH)

    @pl.loop(1, n_row)
    def _(d):
        pl.semaphore_signal(barrier, inc=1, device_id={"row": lax.rem(row + d, n_row)}, device_id_type=MESH)

    g = g_ref[...]
    gf = g.astype(F32)
    local_sq = jnp.sum(gf * gf)
    sq_out[...] = jnp.full((1, 128), local_sq, F32)
    lpart[...] = mm(g, g, NT)
    pl.semaphore_wait(barrier, n_plane - 1 + n_row - 1)

    @pl.loop(1, n_plane)
    def _(q):
        pltpu.make_async_remote_copy(
            src_ref=sq_out, dst_ref=sq_plane.at[q - 1], send_sem=sq_sems.at[0], recv_sem=sq_sems.at[1],
            device_id=plane_peer(q), device_id_type=MESH,
        ).start()

    @pl.loop(1, n_col)
    def _(d):
        other = lax.rem(col + d, n_col)
        pltpu.make_async_remote_copy(
            src_ref=lpart.at[pl.ds(pl.multiple_of(other * bl, bl), bl)], dst_ref=lin.at[d - 1],
            send_sem=l_sems.at[0], recv_sem=l_sems.at[1], device_id={"col": other}, device_id_type=MESH,
        ).start()

    rpart[...] = mm(g, g, TN)

    @pl.loop(1, n_row)
    def _(d):
        other = lax.rem(row + d, n_row)
        pltpu.make_async_remote_copy(
            src_ref=rpart.at[pl.ds(pl.multiple_of(other * br, br), br)], dst_ref=rin.at[d - 1],
            send_sem=r_sems.at[0], recv_sem=r_sems.at[1], device_id={"row": other}, device_id_type=MESH,
        ).start()

    for i in range(left // 128):
        rows = slice(i * 128, (i + 1) * 128)
        half_turn = mm(ql_ref[:, rows], g, TN).astype(BF16)
        rot[rows, :] = mm(half_turn, qr_ref[...])

    pltpu.make_async_copy(sq_plane, sq_plane, sq_sems.at[1]).wait()
    sq_mid[...] = sq_out[...] + jnp.sum(sq_plane[...], axis=0)

    @pl.loop(1, n_row)
    def _(d):
        pltpu.make_async_remote_copy(
            src_ref=sq_mid, dst_ref=sq_line.at[d - 1], send_sem=sq_sems.at[2], recv_sem=sq_sems.at[3],
            device_id={"row": lax.rem(row + d, n_row)}, device_id_type=MESH,
        ).start()

    pltpu.make_async_copy(sq_line, sq_line, sq_sems.at[3]).wait()
    total_sq = (sq_mid[...] + jnp.sum(sq_line[...], axis=0))[:, :1]
    clip = jnp.minimum(1.0, max_norm * lax.rsqrt(total_sq + NORM_EPS))
    clip_sq = clip * clip
    coef_left = (1.0 - STATISTICS_DECAY) * (clip_sq / (right * n_col))
    coef_right = (1.0 - STATISTICS_DECAY) * (clip_sq / (left * n_row))

    pltpu.make_async_copy(lin, lin, l_sems.at[1]).wait()
    mine = pl.ds(pl.multiple_of(col * bl, bl), bl)
    lsum = lpart[mine]
    for d in range(n_col - 1):
        lsum = lsum + lin[d]
    lnew = STATISTICS_DECAY * lold_ref[...] + coef_left * lsum
    lfull[mine] = lnew

    @pl.loop(1, n_col)
    def _(d):
        pltpu.make_async_remote_copy(
            src_ref=lfull.at[mine], dst_ref=lfull.at[mine],
            send_sem=l_sems.at[2], recv_sem=l_sems.at[3],
            device_id={"col": lax.rem(col + d, n_col)}, device_id_type=MESH,
        ).start()

    pltpu.make_async_copy(rin, rin, r_sems.at[1]).wait()
    mine_r = pl.ds(pl.multiple_of(row * br, br), br)
    rsum = rpart[mine_r]
    for d in range(n_row - 1):
        rsum = rsum + rin[d]
    rnew = STATISTICS_DECAY * rold_ref[...] + coef_right * rsum
    rfull[mine_r] = rnew

    @pl.loop(1, n_row)
    def _(d):
        pltpu.make_async_remote_copy(
            src_ref=rfull.at[mine_r], dst_ref=rfull.at[mine_r],
            send_sem=r_sems.at[2], recv_sem=r_sems.at[3],
            device_id={"row": lax.rem(row + d, n_row)}, device_id_type=MESH,
        ).start()

    lnew_ref[...] = lnew
    rnew_ref[...] = rnew
    inv_scale = 1.0 / math.sqrt(left * right)
    turn_scale = clip * inv_scale
    for i in range(left // 64):
        rows = slice(i * 64, (i + 1) * 64)
        rotated = rot[rows, :] * turn_scale
        first = BETA_FIRST * m_ref[rows, :].astype(F32) + (1.0 - BETA_FIRST) * rotated
        second = BETA_SECOND * v_ref[rows, :].astype(F32) + (1.0 - BETA_SECOND) * rotated * rotated
        first_ref[rows, :] = first.astype(BF16)
        second_ref[rows, :] = second.astype(BF16)
        direction[rows, :] = (first / (jnp.sqrt(second) + ADAM_EPS)).astype(BF16)
    for i in range(left // 128):
        rows = slice(i * 128, (i + 1) * 128)
        back_half = mm(ql_ref[rows, :], direction[...]).astype(BF16)
        upd_ref[rows, :] = (mm(back_half, qr_ref[...], NT) * inv_scale).astype(BF16)

    rest = lfull.at[pl.ds(0, left - bl)]
    pltpu.make_async_copy(rest, rest, l_sems.at[3]).wait()
    out_l = pltpu.make_async_copy(lfull, lfull_out, out_sems.at[0])
    out_l.start()
    rest_r = rfull.at[pl.ds(0, right - br)]
    pltpu.make_async_copy(rest_r, rest_r, r_sems.at[3]).wait()
    out_r = pltpu.make_async_copy(rfull, rfull_out, out_sems.at[1])
    out_r.start()
    pltpu.make_async_copy(sq_plane, sq_plane, sq_sems.at[0]).wait()
    pltpu.make_async_copy(sq_line, sq_line, sq_sems.at[2]).wait()
    pltpu.make_async_copy(lin, lin, l_sems.at[0]).wait()
    pltpu.make_async_copy(rin, rin, r_sems.at[0]).wait()
    pltpu.make_async_copy(rest, rest, l_sems.at[2]).wait()
    pltpu.make_async_copy(rest_r, rest_r, r_sems.at[2]).wait()
    out_l.wait()
    out_r.wait()


def refresh_kernel(l_ref, r_ref, ql_ref, qr_ref, *refs):
    count = (len(refs) - 5) // 2
    kept_in, (bl_ref, br_ref), kept_out, (xl, xr, sems) = (
        refs[:count], refs[count:count + 2], refs[count + 2:2 * count + 2], refs[2 * count + 2:]
    )
    copies = [
        pltpu.make_async_copy(src, dst, sems.at[k]) for k, (src, dst) in enumerate(zip(kept_in, kept_out))
    ]
    for copy in copies:
        copy.start()

    def start(stats_ref, basis_ref, x_ref):
        hi, lo = halves(stats_ref[...])
        product = mm(hi, basis_ref[...]) + mm(lo, basis_ref[...])
        x_ref[...] = product * lax.rsqrt(jnp.sum(product * product) + NORM_EPS)

    def step(x_ref):
        x = x_ref[...]
        parts = halves(x)
        gram = mm3(parts, parts, NT)
        gram_parts = halves(gram)
        poly = NS_COEFFS[1] * gram + NS_COEFFS[2] * mm3(gram_parts, gram_parts)
        x_ref[...] = NS_COEFFS[0] * x + mm3(halves(poly), parts)

    start(l_ref, ql_ref, xl)
    start(r_ref, qr_ref, xr)

    @pl.loop(0, NS_STEPS)
    def _(_):
        step(xl)
        step(xr)

    bl_ref[...] = (xl[...] * math.sqrt(xl.shape[0])).astype(BF16)
    br_ref[...] = (xr[...] * math.sqrt(xr.shape[0])).astype(BF16)
    for copy in copies:
        copy.wait()


def local(grad, exp_avg, exp_avg_sq, left_basis, right_basis, left_stats, right_stats, sizes):
    n_row, n_col, n_grp, _ = sizes
    args = [x[0] for x in (grad, exp_avg, exp_avg_sq, left_basis, right_basis)]
    args += [left_stats[0].T, right_stats[0].T]
    left, right = args[0].shape
    bl, br = left // n_col, right // n_row
    vmem = pl.BlockSpec(memory_space=pltpu.VMEM)
    anywhere = pl.BlockSpec(memory_space=pl.ANY)
    tile = jax.ShapeDtypeStruct((left, right), BF16)
    shape = jax.ShapeDtypeStruct
    upd, first, second, lfull, rfull, lnew, rnew = pl.pallas_call(
        functools.partial(exchange_kernel, sizes),
        out_shape=[tile, tile, tile, shape((left, left), F32), shape((right, right), F32),
                   shape((bl, left), F32), shape((br, right), F32)],
        in_specs=[vmem] * 7,
        out_specs=[vmem] * 3 + [anywhere] * 2 + [vmem] * 2,
        scratch_shapes=[
            pltpu.VMEM((left, left), F32),
            pltpu.VMEM((right, right), F32),
            pltpu.VMEM((n_col - 1, bl, left), F32),
            pltpu.VMEM((n_row - 1, br, right), F32),
            pltpu.VMEM((left, left), F32),
            pltpu.VMEM((right, right), F32),
            pltpu.VMEM((1, 128), F32),
            pltpu.VMEM((n_col * n_grp - 1, 1, 128), F32),
            pltpu.VMEM((1, 128), F32),
            pltpu.VMEM((n_row - 1, 1, 128), F32),
            pltpu.VMEM((left, right), F32),
            pltpu.VMEM((left, right), BF16),
            pltpu.SemaphoreType.DMA((4,)),
            pltpu.SemaphoreType.DMA((4,)),
            pltpu.SemaphoreType.DMA((4,)),
            pltpu.SemaphoreType.DMA((2,)),
        ],
        compiler_params=pltpu.CompilerParams(
            collective_id=0, has_side_effects=True, vmem_limit_bytes=32 * 1024 * 1024
        ),
        name="exchange",
    )(*args)
    kept = [upd, first, second, lnew, rnew]
    new_left, new_right, upd, first, second, lnew, rnew = pl.pallas_call(
        refresh_kernel,
        out_shape=[shape((left, left), BF16), shape((right, right), BF16)]
        + [shape(x.shape, x.dtype) for x in kept],
        in_specs=[vmem] * 4 + [anywhere] * 5,
        out_specs=[vmem] * 2 + [anywhere] * 5,
        scratch_shapes=[
            pltpu.VMEM((left, left), F32),
            pltpu.VMEM((right, right), F32),
            pltpu.SemaphoreType.DMA((5,)),
        ],
        compiler_params=pltpu.CompilerParams(vmem_limit_bytes=32 * 1024 * 1024),
        name="refresh",
    )(lfull, rfull, args[3], args[4], *kept)
    return tuple(x[None] for x in (upd, first, second, new_left, new_right, lnew.T, rnew.T))


def solution(mesh):
    n_row, n_col, n_grp = mesh.shape["row"], mesh.shape["col"], mesh.shape["grp"]
    tiled = P("grp", "row", "col")
    by_row, by_col = P("grp", "row", None), P("grp", "col", None)
    turned_tiles = P("grp", "col", "row")

    def step(grad, *rest):
        sizes = (n_row, n_col, n_grp, math.sqrt(grad.size))
        return jax.shard_map(
            functools.partial(local, sizes=sizes),
            mesh=mesh,
            in_specs=(tiled, tiled, tiled, by_row, by_col, tiled, turned_tiles),
            out_specs=(tiled, tiled, tiled, by_row, by_col, tiled, turned_tiles),
            check_vma=False,
        )(grad, *rest)

    return step
```

```python
import functools
import math

import jax
import jax.numpy as jnp
from jax import lax
from jax.experimental import pallas as pl
from jax.experimental.pallas import tpu as pltpu
from jax.sharding import PartitionSpec as P

NS_STEPS = 3
NS_COEFFS = (3.4445, -4.775, 2.0315)
BETA_FIRST = 0.9
BETA_SECOND = 0.99
STATISTICS_DECAY = 0.95
ADAM_EPS = 1e-08
NORM_EPS = 1e-06
F32 = jnp.float32
BF16 = jnp.bfloat16
MESH = pl.DeviceIdType.MESH
NN = (((1,), (0,)), ((), ()))
NT = (((1,), (1,)), ((), ()))
TN = (((0,), (0,)), ((), ()))


def mm(a, b, dims=NN):
    return lax.dot_general(a, b, dims, preferred_element_type=F32)


def halves(x):
    hi = x.astype(BF16)
    return hi, (x - hi.astype(F32)).astype(BF16)


def mm3(a, b, dims=NN):
    return mm(a[0], b[0], dims) + (mm(a[0], b[1], dims) + mm(a[1], b[0], dims))


def packed_far(far, block):
    rows = block * block // 128
    lane = lax.broadcasted_iota(jnp.int32, (rows, 128), 1)
    out = far[:rows]
    for k in range(1, 128 // block):
        out = jnp.where(lane >= k * block, far[k * rows:(k + 1) * rows], out)
    return out


def unpacked_far(packed, block):
    rows = block * block // 128
    lane = lax.broadcasted_iota(jnp.int32, (rows, 128), 1)
    parts = [packed] + [pltpu.roll(packed, 128 - k * block, 1) for k in range(1, 128 // block)]
    return jnp.concatenate([jnp.where(lane < block, part, 0.0) for part in parts], 0)


def step_kernel(
    sizes,
    g_hbm, m_hbm, v_hbm, ql_hbm, qr_hbm, lold_hbm, rold_hbm,
    upd_ref, first_ref, second_ref, newl_ref, newr_ref, lnew_ref, rnew_ref,
    twice, m_ref, v_ref, ql_ref, qr_ref, lold_ref, rold_ref,
    lpart, lin, lgather, lhalf, lfull, rpart, rin, rfull,
    sq_out, sq_line, sq_mid, sq_plane, rot, direction, xl, xr,
    in_sems, sq_sems, l_sems, r_sems,
):
    n_row, n_col, n_grp, max_norm = sizes
    left, right = g_hbm.shape
    bl, br = left // n_col, right // n_row
    far_rows = bl * bl // 128
    row, col, grp = lax.axis_index("row"), lax.axis_index("col"), lax.axis_index("grp")
    n_plane = n_col * n_grp
    place = col * n_grp + grp

    def row_peer(d):
        return {"row": lax.rem(row + d, n_row)}

    def col_peer(d):
        return {"col": lax.rem(col + d, n_col)}

    def plane_peer(q):
        other = lax.rem(place + q, n_plane)
        return {"col": other // n_grp, "grp": lax.rem(other, n_grp)}

    def remote(src, dst, sems, k, peer):
        return pltpu.make_async_remote_copy(
            src_ref=src, dst_ref=dst, send_sem=sems.at[k], recv_sem=sems.at[k + 1],
            device_id=peer, device_id_type=MESH,
        )

    def wait(ref, sem):
        pltpu.make_async_copy(ref, ref, sem).wait()

    fetched = [
        pltpu.make_async_copy(src, dst, in_sems.at[k])
        for k, (src, dst) in enumerate([
            (g_hbm, twice.at[pl.ds(0, left)]), (g_hbm, twice.at[pl.ds(left, left)]),
            (ql_hbm, ql_ref), (qr_hbm, qr_ref), (m_hbm, m_ref), (v_hbm, v_ref),
            (lold_hbm, lold_ref), (rold_hbm, rold_ref),
        ])
    ]
    for copy in fetched:
        copy.start()
    barrier = pltpu.get_barrier_semaphore()

    @pl.loop(1, n_row)
    def _(d):
        pl.semaphore_signal(barrier, inc=1, device_id=row_peer(d), device_id_type=MESH)

    @pl.loop(1, n_plane)
    def _(q):
        pl.semaphore_signal(barrier, inc=1, device_id=plane_peer(q), device_id_type=MESH)

    fetched[0].wait()
    fetched[1].wait()
    g = twice[:left]
    gf = g.astype(F32)
    sq_out[...] = jnp.full((1, 128), jnp.sum(gf * gf), F32)

    @pl.loop(0, n_col)
    def _(t):
        begin = pl.multiple_of(t * bl, bl)
        far = twice[pl.ds(pl.multiple_of(begin + left // 2, bl), bl)]
        others = jnp.concatenate([twice[pl.ds(begin, left // 2)]] + [far] * (128 // bl), 0)
        products = mm(twice[pl.ds(begin, bl)], others, NT)
        for k in range(left // 256):
            lpart[t, k * bl:(k + 1) * bl] = products[:, k * 128:(k + 1) * 128]
        lpart[t, (left // 256) * bl:] = packed_far(products[:, left // 2:], bl)

    rpart[...] = mm(g, g, TN)
    pl.semaphore_wait(barrier, n_plane - 1 + n_row - 1)

    @pl.loop(1, n_row)
    def _(d):
        remote(sq_out, sq_line.at[d - 1], sq_sems, 0, row_peer(d)).start()

    @pl.loop(1, n_col)
    def _(d):
        other = lax.rem(col + d, n_col)
        remote(lpart.at[other], lin.at[d - 1], l_sems, 0, {"col": other}).start()

    @pl.loop(1, n_row)
    def _(d):
        other = lax.rem(row + d, n_row)
        theirs = rpart.at[pl.ds(pl.multiple_of(other * br, br), br)]
        remote(theirs, rin.at[d - 1], r_sems, 0, {"row": other}).start()

    for copy in fetched[2:]:
        copy.wait()
    for i in range(left // 256):
        rows = slice(i * 256, (i + 1) * 256)
        half_turn = mm(ql_ref[:, rows], g, TN).astype(BF16)
        rot[rows, :] = mm(half_turn, qr_ref[...])

    wait(sq_line, sq_sems.at[1])
    sq_mid[...] = sq_out[...] + jnp.sum(sq_line[...], axis=0)

    @pl.loop(1, n_plane)
    def _(q):
        remote(sq_mid, sq_plane.at[q - 1], sq_sems, 2, plane_peer(q)).start()

    lold = pltpu.roll(lold_ref[...], lax.rem(left - col * bl, left), 1)
    lane = lax.broadcasted_iota(jnp.int32, (bl, 128), 1)
    far = jnp.where(lane < bl, lold[:, left // 2:left // 2 + 128], 0.0)
    spread = far
    for k in range(1, 128 // bl):
        spread = spread + pltpu.roll(far, k * bl, 1)
    lold = jnp.concatenate(
        [lold[:, k * 128:(k + 1) * 128] for k in range(left // 256)] + [packed_far(spread, bl)], 0
    )

    wait(sq_plane, sq_sems.at[3])
    total_sq = (sq_mid[...] + jnp.sum(sq_plane[...], axis=0))[:, :1]
    clip = jnp.minimum(1.0, max_norm * lax.rsqrt(total_sq + NORM_EPS))
    clip_sq = clip * clip
    coef_left = (1.0 - STATISTICS_DECAY) * (clip_sq / (right * n_col))
    coef_right = (1.0 - STATISTICS_DECAY) * (clip_sq / (left * n_row))

    wait(lin, l_sems.at[1])
    lsum = lpart[col]
    for d in range(n_col - 1):
        lsum = lsum + lin[d]
    lgather[col] = STATISTICS_DECAY * lold + coef_left * lsum

    @pl.loop(1, n_col)
    def _(d):
        remote(lgather.at[col], lgather.at[col], l_sems, 2, col_peer(d)).start()

    wait(rin, r_sems.at[1])
    mine = pl.ds(pl.multiple_of(row * br, br), br)
    rsum = rpart[mine]
    for d in range(n_row - 1):
        rsum = rsum + rin[d]
    rnew = STATISTICS_DECAY * rold_ref[...] + coef_right * rsum
    rfull[mine] = rnew

    @pl.loop(1, n_row)
    def _(d):
        remote(rfull.at[mine], rfull.at[mine], r_sems, 2, row_peer(d)).start()

    rnew_ref[...] = rnew
    inv_scale = 1.0 / math.sqrt(left * right)
    turn_scale = clip * inv_scale
    for i in range(left // 64):
        rows = slice(i * 64, (i + 1) * 64)
        rotated = rot[rows, :] * turn_scale
        first = BETA_FIRST * m_ref[rows, :].astype(F32) + (1.0 - BETA_FIRST) * rotated
        second = BETA_SECOND * v_ref[rows, :].astype(F32) + (1.0 - BETA_SECOND) * rotated * rotated
        first_ref[rows, :] = first.astype(BF16)
        second_ref[rows, :] = second.astype(BF16)
        direction[rows, :] = (first / (jnp.sqrt(second) + ADAM_EPS)).astype(BF16)
    for i in range(left // 256):
        rows = slice(i * 256, (i + 1) * 256)
        back_half = mm(ql_ref[rows, :], direction[...]).astype(BF16)
        upd_ref[rows, :] = (mm(back_half, qr_ref[...], NT) * inv_scale).astype(BF16)

    wait(lgather.at[pl.ds(0, n_col - 1)], l_sems.at[3])
    for t in range(n_col):
        slab = lgather[t]
        wide = [slab[k * bl:(k + 1) * bl] for k in range(left // 256)]
        wide.append(unpacked_far(slab[(left // 256) * bl:], bl))
        wide.append(jnp.zeros((bl, left // 2 - 128), F32))
        lhalf[t * bl:(t + 1) * bl, :] = pltpu.roll(jnp.concatenate(wide, 1), t * bl, 1)
    shift = bl.bit_length() - 1
    for i in range(left // 128):
        for j in range(left // 128):
            r = lax.broadcasted_iota(jnp.int32, (128, 128), 0) + i * 128
            c = lax.broadcasted_iota(jnp.int32, (128, 128), 1) + j * 128
            held = (((c >> shift) - (r >> shift)) & (n_col - 1)) <= n_col // 2
            here, there = slice(i * 128, (i + 1) * 128), slice(j * 128, (j + 1) * 128)
            lfull[here, there] = jnp.where(held, lhalf[here, there], lhalf[there, here].T)
    lnew_ref[...] = lfull[pl.ds(pl.multiple_of(col * bl, bl), bl)]

    def start(stats_ref, basis_ref, x_ref):
        hi, lo = halves(stats_ref[...])
        product = mm(hi, basis_ref[...]) + mm(lo, basis_ref[...])
        x_ref[...] = product * lax.rsqrt(jnp.sum(product * product) + NORM_EPS)

    def refine(x_ref):
        x = x_ref[...]
        parts = halves(x)
        gram = mm3(parts, parts, NT)
        gram_parts = halves(gram)
        poly = NS_COEFFS[1] * gram + NS_COEFFS[2] * mm3(gram_parts, gram_parts)
        x_ref[...] = NS_COEFFS[0] * x + mm3(halves(poly), parts)

    start(lfull, ql_ref, xl)
    rest = rfull.at[pl.ds(0, right - br)]
    wait(rest, r_sems.at[3])
    start(rfull, qr_ref, xr)

    @pl.loop(0, NS_STEPS)
    def _(_):
        refine(xl)
        refine(xr)

    newl_ref[...] = (xl[...] * math.sqrt(left)).astype(BF16)
    newr_ref[...] = (xr[...] * math.sqrt(right)).astype(BF16)
    wait(sq_line, sq_sems.at[0])
    wait(sq_plane, sq_sems.at[2])
    wait(lin, l_sems.at[0])
    wait(lgather.at[pl.ds(0, n_col - 1)], l_sems.at[2])
    wait(rin, r_sems.at[0])
    wait(rest, r_sems.at[2])


def finish_kernel(*refs):
    count = (len(refs) - 1) // 2
    copies = [pltpu.make_async_copy(refs[k], refs[count + k], refs[-1].at[k]) for k in range(count)]
    for copy in copies:
        copy.start()
    for copy in copies:
        copy.wait()


def local(grad, exp_avg, exp_avg_sq, left_basis, right_basis, left_stats, right_stats, sizes):
    n_row, n_col, n_grp, _ = sizes
    args = [x[0] for x in (grad, exp_avg, exp_avg_sq, left_basis, right_basis)]
    args += [left_stats[0].T, right_stats[0].T]
    left, right = args[0].shape
    bl, br = left // n_col, right // n_row
    wire = (left // 256) * bl + bl * bl // 128
    in_hbm = pl.BlockSpec(memory_space=pltpu.HBM)
    in_vmem = pl.BlockSpec(memory_space=pltpu.VMEM)
    outs = [((left, right), BF16)] * 3 + [
        ((left, left), BF16), ((right, right), BF16), ((bl, left), F32), ((br, right), F32)
    ]
    results = pl.pallas_call(
        functools.partial(step_kernel, sizes),
        out_shape=[pltpu.VMEM(shape, dtype) for shape, dtype in outs],
        in_specs=[in_hbm] * len(args),
        out_specs=[in_vmem] * len(outs),
        scratch_shapes=[
            pltpu.VMEM((2 * left, right), BF16),
            *[pltpu.VMEM(x.shape, x.dtype) for x in args[1:]],
            pltpu.VMEM((n_col, wire, 128), F32),
            pltpu.VMEM((n_col - 1, wire, 128), F32),
            pltpu.VMEM((n_col, wire, 128), F32),
            pltpu.VMEM((left, left), F32),
            pltpu.VMEM((left, left), F32),
            pltpu.VMEM((right, right), F32),
            pltpu.VMEM((n_row - 1, br, right), F32),
            pltpu.VMEM((right, right), F32),
            pltpu.VMEM((1, 128), F32),
            pltpu.VMEM((n_row - 1, 1, 128), F32),
            pltpu.VMEM((1, 128), F32),
            pltpu.VMEM((n_col * n_grp - 1, 1, 128), F32),
            pltpu.VMEM((left, right), F32),
            pltpu.VMEM((left, right), BF16),
            pltpu.VMEM((left, left), F32),
            pltpu.VMEM((right, right), F32),
            pltpu.SemaphoreType.DMA((8,)),
            pltpu.SemaphoreType.DMA((4,)),
            pltpu.SemaphoreType.DMA((4,)),
            pltpu.SemaphoreType.DMA((4,)),
        ],
        compiler_params=pltpu.CompilerParams(
            collective_id=0, has_side_effects=True, vmem_limit_bytes=40 * 1024 * 1024
        ),
        name="step",
    )(*[pltpu.with_memory_space_constraint(x, pltpu.HBM) for x in args])
    results = pl.pallas_call(
        finish_kernel,
        out_shape=[pltpu.HBM(shape, dtype) for shape, dtype in outs],
        in_specs=[in_vmem] * len(outs),
        out_specs=[in_hbm] * len(outs),
        scratch_shapes=[pltpu.SemaphoreType.DMA((len(outs),))],
        name="finish",
    )(*[pltpu.with_memory_space_constraint(x, pltpu.VMEM) for x in results])
    results = [*results[:5], results[5].T, results[6].T]
    return tuple(x[None] for x in results)


def solution(mesh):
    n_row, n_col, n_grp = mesh.shape["row"], mesh.shape["col"], mesh.shape["grp"]
    tiled = P("grp", "row", "col")
    by_row, by_col = P("grp", "row", None), P("grp", "col", None)
    turned_tiles = P("grp", "col", "row")

    def step(grad, *rest):
        sizes = (n_row, n_col, n_grp, math.sqrt(grad.size))
        return jax.shard_map(
            functools.partial(local, sizes=sizes),
            mesh=mesh,
            in_specs=(tiled, tiled, tiled, by_row, by_col, tiled, turned_tiles),
            out_specs=(tiled, tiled, tiled, by_row, by_col, tiled, turned_tiles),
            check_vma=False,
        )(grad, *rest)

    return step
```

```python
import functools
import math

import jax
import jax.numpy as jnp
from jax import lax
from jax.experimental import pallas as pl
from jax.experimental.pallas import tpu as pltpu
from jax.sharding import PartitionSpec as P

NS_STEPS = 3
NS_COEFFS = (3.4445, -4.775, 2.0315)
BETA_FIRST = 0.9
BETA_SECOND = 0.99
STATISTICS_DECAY = 0.95
ADAM_EPS = 1e-08
NORM_EPS = 1e-06
F32 = jnp.float32
BF16 = jnp.bfloat16
MESH = pl.DeviceIdType.MESH
NN = (((1,), (0,)), ((), ()))
NT = (((1,), (1,)), ((), ()))
TN = (((0,), (0,)), ((), ()))


def mm(a, b, dims=NN):
    return lax.dot_general(a, b, dims, preferred_element_type=F32)


def halves(x):
    hi = x.astype(BF16)
    return hi, (x - hi.astype(F32)).astype(BF16)


def mm3(a, b, dims=NN):
    return mm(a[0], b[0], dims) + (mm(a[0], b[1], dims) + mm(a[1], b[0], dims))


def wire_rows(size, count):
    block = size // count
    return size // 256 * block + block * block // 128


def to_wire(rows, out):
    block, size = rows.shape
    for k in range(size // 256):
        out[k * block:(k + 1) * block] = rows[:, k * 128:(k + 1) * 128]
    fold = block * block // 128
    far = rows[:, size // 2:size // 2 + 128]
    lane = lax.broadcasted_iota(jnp.int32, (fold, 128), 1)
    folded = far[:fold]
    for k in range(1, 128 // block):
        folded = jnp.where(lane >= k * block, pltpu.roll(far[k * fold:(k + 1) * fold], k * block, 1), folded)
    out[size // 256 * block:] = folded


def from_wire(wire, size, block):
    fold = block * block // 128
    folded = wire[size // 256 * block:]
    lane = lax.broadcasted_iota(jnp.int32, (fold, 128), 1)
    far = [folded] + [pltpu.roll(folded, 128 - k * block, 1) for k in range(1, 128 // block)]
    wide = [wire[k * block:(k + 1) * block] for k in range(size // 256)]
    wide.append(jnp.concatenate([jnp.where(lane < block, part, 0.0) for part in far], 0))
    if size > 256:
        wide.append(jnp.zeros((block, size // 2 - 128), F32))
    return jnp.concatenate(wide, 1)


def pack_all(square, wires):
    count = wires.shape[0]
    size = square.shape[0]
    block = size // count
    for t in range(count):
        rows = square[t * block:(t + 1) * block, :]
        to_wire(pltpu.roll(rows, (size - t * block) % size, 1), wires.at[t])


def unpack_all(wires, half, square):
    count = wires.shape[0]
    size = square.shape[0]
    block = size // count
    for t in range(count):
        half[t * block:(t + 1) * block, :] = pltpu.roll(from_wire(wires[t], size, block), t * block, 1)
    shift = block.bit_length() - 1
    for i in range(size // 128):
        for j in range(size // 128):
            r = lax.broadcasted_iota(jnp.int32, (128, 128), 0) + i * 128
            c = lax.broadcasted_iota(jnp.int32, (128, 128), 1) + j * 128
            held = (((c >> shift) - (r >> shift)) & (count - 1)) <= count // 2
            here, there = slice(i * 128, (i + 1) * 128), slice(j * 128, (j + 1) * 128)
            square[here, there] = jnp.where(held, half[here, there], half[there, here].T)


def part(k):
    return slice(k * 256, (k + 1) * 256)


def square_part(hi, lo, i, j):
    if i == j:
        cross = mm(hi[part(i), :], lo[part(i), :], NT)
        return mm(hi[part(i), :], hi[part(i), :], NT) + (cross + cross.T)
    return mm3((hi[part(i), :], lo[part(i), :]), (hi[part(j), :], lo[part(j), :]), NT)


def refine(x, x_hi, x_lo, poly, gram_hi, gram_lo):
    count = x.shape[0] // 256
    upper = [(i, j) for i in range(count) for j in range(i, count)]
    for i in range(count):
        x_hi[part(i), :], x_lo[part(i), :] = halves(x[part(i), :])
    for i, j in upper:
        gram = square_part(x_hi, x_lo, i, j)
        poly[part(i), part(j)] = gram
        gram_hi[part(i), part(j)], gram_lo[part(i), part(j)] = halves(gram)
        if i != j:
            gram_hi[part(j), part(i)], gram_lo[part(j), part(i)] = halves(gram.T)
    for i, j in upper:
        block = NS_COEFFS[1] * poly[part(i), part(j)] + NS_COEFFS[2] * square_part(gram_hi, gram_lo, i, j)
        poly[part(i), part(j)] = block
        if i != j:
            poly[part(j), part(i)] = block.T
    for i in range(count):
        product = mm3(halves(poly[part(i), :]), (x_hi[...], x_lo[...]))
        x[part(i), :] = NS_COEFFS[0] * x[part(i), :] + product


def step_kernel(
    sizes,
    g_hbm, m_hbm, v_hbm, ql_hbm, qr_hbm, lold_hbm, rold_hbm,
    upd_ref, first_ref, second_ref, newl_ref, newr_ref, lnew_ref, rnew_ref,
    g_ref, m_ref, v_ref, ql_ref, qr_ref, lold_ref, rold_ref,
    lpart, lin, lgather, lhalf, lfull, rpart, rin, rgather, rhalf, rfull,
    sq_out, sq_line, sq_mid, sq_plane, rot, direction, xl, xr,
    l_hi, l_lo, l_poly, lg_hi, lg_lo, r_hi, r_lo, r_poly, rg_hi, rg_lo,
    in_sems, sq_sems, l_sems, r_sems,
):
    n_row, n_col, n_grp, max_norm = sizes
    left, right = g_hbm.shape
    bl, br = left // n_col, right // n_row
    row, col, grp = lax.axis_index("row"), lax.axis_index("col"), lax.axis_index("grp")
    n_plane = n_col * n_grp
    place = col * n_grp + grp

    def row_peer(d):
        return {"row": lax.rem(row + d, n_row)}

    def col_peer(d):
        return {"col": lax.rem(col + d, n_col)}

    def plane_peer(q):
        other = lax.rem(place + q, n_plane)
        return {"col": other // n_grp, "grp": lax.rem(other, n_grp)}

    def remote(src, dst, sems, k, peer):
        return pltpu.make_async_remote_copy(
            src_ref=src, dst_ref=dst, send_sem=sems.at[k], recv_sem=sems.at[k + 1],
            device_id=peer, device_id_type=MESH,
        )

    def wait(ref, sem):
        pltpu.make_async_copy(ref, ref, sem).wait()

    fetched = [
        pltpu.make_async_copy(src, dst, in_sems.at[k])
        for k, (src, dst) in enumerate([
            (g_hbm, g_ref), (ql_hbm, ql_ref), (qr_hbm, qr_ref), (m_hbm, m_ref), (v_hbm, v_ref),
            (lold_hbm, lold_ref), (rold_hbm, rold_ref),
        ])
    ]
    for copy in fetched:
        copy.start()
    barrier = pltpu.get_barrier_semaphore()

    @pl.loop(1, n_row)
    def _(d):
        pl.semaphore_signal(barrier, inc=1, device_id=row_peer(d), device_id_type=MESH)

    @pl.loop(1, n_plane)
    def _(q):
        pl.semaphore_signal(barrier, inc=1, device_id=plane_peer(q), device_id_type=MESH)

    fetched[0].wait()
    g = g_ref[...]
    gf = g.astype(F32)
    sq_out[...] = jnp.full((1, 128), jnp.sum(gf * gf), F32)
    lfull[...] = mm(g, g, NT)
    pack_all(lfull, lpart)
    rfull[...] = mm(g, g, TN)
    pack_all(rfull, rpart)
    pl.semaphore_wait(barrier, n_plane - 1 + n_row - 1)

    @pl.loop(1, n_row)
    def _(d):
        remote(sq_out, sq_line.at[d - 1], sq_sems, 0, row_peer(d)).start()

    @pl.loop(1, n_col)
    def _(d):
        other = lax.rem(col + d, n_col)
        remote(lpart.at[other], lin.at[d - 1], l_sems, 0, {"col": other}).start()

    @pl.loop(1, n_row)
    def _(d):
        other = lax.rem(row + d, n_row)
        remote(rpart.at[other], rin.at[d - 1], r_sems, 0, {"row": other}).start()

    wait(sq_line, sq_sems.at[1])
    sq_mid[...] = sq_out[...] + jnp.sum(sq_line[...], axis=0)

    @pl.loop(1, n_plane)
    def _(q):
        remote(sq_mid, sq_plane.at[q - 1], sq_sems, 2, plane_peer(q)).start()

    for copy in fetched[1:]:
        copy.wait()
    for i in range(left // 256):
        rows = part(i)
        half_turn = mm(ql_ref[:, rows], g, TN).astype(BF16)
        rot[rows, :] = mm(half_turn, qr_ref[...])

    to_wire(pltpu.roll(lold_ref[...], lax.rem(left - col * bl, left), 1), lgather.at[col])
    to_wire(pltpu.roll(rold_ref[...], lax.rem(right - row * br, right), 1), rgather.at[row])

    wait(sq_plane, sq_sems.at[3])
    total_sq = (sq_mid[...] + jnp.sum(sq_plane[...], axis=0))[:, :1]
    clip = jnp.minimum(1.0, max_norm * lax.rsqrt(total_sq + NORM_EPS))
    clip_sq = clip * clip
    coef_left = (1.0 - STATISTICS_DECAY) * (clip_sq / (right * n_col))
    coef_right = (1.0 - STATISTICS_DECAY) * (clip_sq / (left * n_row))

    wait(lin, l_sems.at[1])
    lsum = lpart[col]
    for d in range(n_col - 1):
        lsum = lsum + lin[d]
    lgather[col] = STATISTICS_DECAY * lgather[col] + coef_left * lsum

    @pl.loop(1, n_col)
    def _(d):
        remote(lgather.at[col], lgather.at[col], l_sems, 2, col_peer(d)).start()

    wait(rin, r_sems.at[1])
    rsum = rpart[row]
    for d in range(n_row - 1):
        rsum = rsum + rin[d]
    rgather[row] = STATISTICS_DECAY * rgather[row] + coef_right * rsum

    @pl.loop(1, n_row)
    def _(d):
        remote(rgather.at[row], rgather.at[row], r_sems, 2, row_peer(d)).start()

    inv_scale = 1.0 / math.sqrt(left * right)
    turn_scale = clip * inv_scale
    for i in range(left // 64):
        rows = slice(i * 64, (i + 1) * 64)
        rotated = rot[rows, :] * turn_scale
        first = BETA_FIRST * m_ref[rows, :].astype(F32) + (1.0 - BETA_FIRST) * rotated
        second = BETA_SECOND * v_ref[rows, :].astype(F32) + (1.0 - BETA_SECOND) * rotated * rotated
        first_ref[rows, :] = first.astype(BF16)
        second_ref[rows, :] = second.astype(BF16)
        direction[rows, :] = (first / (jnp.sqrt(second) + ADAM_EPS)).astype(BF16)
    for i in range(left // 256):
        rows = part(i)
        back_half = mm(ql_ref[rows, :], direction[...]).astype(BF16)
        upd_ref[rows, :] = (mm(back_half, qr_ref[...], NT) * inv_scale).astype(BF16)

    def start(stats_ref, basis_ref, x_ref):
        hi, lo = halves(stats_ref[...])
        product = mm(hi, basis_ref[...]) + mm(lo, basis_ref[...])
        x_ref[...] = product * lax.rsqrt(jnp.sum(product * product) + NORM_EPS)

    wait(lgather.at[pl.ds(0, n_col - 1)], l_sems.at[3])
    unpack_all(lgather, lhalf, lfull)
    lnew_ref[...] = lfull[pl.ds(pl.multiple_of(col * bl, bl), bl)]
    start(lfull, ql_ref, xl)
    wait(rgather.at[pl.ds(0, n_row - 1)], r_sems.at[3])
    unpack_all(rgather, rhalf, rfull)
    rnew_ref[...] = rfull[pl.ds(pl.multiple_of(row * br, br), br)]
    start(rfull, qr_ref, xr)

    @pl.loop(0, NS_STEPS)
    def _(_):
        refine(xl, l_hi, l_lo, l_poly, lg_hi, lg_lo)
        refine(xr, r_hi, r_lo, r_poly, rg_hi, rg_lo)

    newl_ref[...] = (xl[...] * math.sqrt(left)).astype(BF16)
    newr_ref[...] = (xr[...] * math.sqrt(right)).astype(BF16)
    wait(sq_line, sq_sems.at[0])
    wait(sq_plane, sq_sems.at[2])
    wait(lin, l_sems.at[0])
    wait(lgather.at[pl.ds(0, n_col - 1)], l_sems.at[2])
    wait(rin, r_sems.at[0])
    wait(rgather.at[pl.ds(0, n_row - 1)], r_sems.at[2])


def finish_kernel(*refs):
    count = (len(refs) - 1) // 2
    copies = [pltpu.make_async_copy(refs[k], refs[count + k], refs[-1].at[k]) for k in range(count)]
    for copy in copies:
        copy.start()
    for copy in copies:
        copy.wait()


def local(grad, exp_avg, exp_avg_sq, left_basis, right_basis, left_stats, right_stats, sizes):
    n_row, n_col, n_grp, _ = sizes
    args = [x[0] for x in (grad, exp_avg, exp_avg_sq, left_basis, right_basis)]
    args += [left_stats[0].T, right_stats[0].T]
    left, right = args[0].shape
    bl, br = left // n_col, right // n_row
    l_wire, r_wire = wire_rows(left, n_col), wire_rows(right, n_row)
    in_hbm = pl.BlockSpec(memory_space=pltpu.HBM)
    in_vmem = pl.BlockSpec(memory_space=pltpu.VMEM)
    outs = [((left, right), BF16)] * 3 + [
        ((left, left), BF16), ((right, right), BF16), ((bl, left), F32), ((br, right), F32)
    ]
    results = pl.pallas_call(
        functools.partial(step_kernel, sizes),
        out_shape=[pltpu.VMEM(shape, dtype) for shape, dtype in outs],
        in_specs=[in_hbm] * len(args),
        out_specs=[in_vmem] * len(outs),
        scratch_shapes=[
            *[pltpu.VMEM(x.shape, x.dtype) for x in args],
            pltpu.VMEM((n_col, l_wire, 128), F32),
            pltpu.VMEM((n_col - 1, l_wire, 128), F32),
            pltpu.VMEM((n_col, l_wire, 128), F32),
            pltpu.VMEM((left, left), F32),
            pltpu.VMEM((left, left), F32),
            pltpu.VMEM((n_row, r_wire, 128), F32),
            pltpu.VMEM((n_row - 1, r_wire, 128), F32),
            pltpu.VMEM((n_row, r_wire, 128), F32),
            pltpu.VMEM((right, right), F32),
            pltpu.VMEM((right, right), F32),
            pltpu.VMEM((1, 128), F32),
            pltpu.VMEM((n_row - 1, 1, 128), F32),
            pltpu.VMEM((1, 128), F32),
            pltpu.VMEM((n_col * n_grp - 1, 1, 128), F32),
            pltpu.VMEM((left, right), F32),
            pltpu.VMEM((left, right), BF16),
            pltpu.VMEM((left, left), F32),
            pltpu.VMEM((right, right), F32),
            *[pltpu.VMEM((size, size), dtype) for size in (left, right) for dtype in (BF16, BF16, F32, BF16, BF16)],
            pltpu.SemaphoreType.DMA((7,)),
            pltpu.SemaphoreType.DMA((4,)),
            pltpu.SemaphoreType.DMA((4,)),
            pltpu.SemaphoreType.DMA((4,)),
        ],
        compiler_params=pltpu.CompilerParams(
            collective_id=0, has_side_effects=True, vmem_limit_bytes=40 * 1024 * 1024
        ),
        name="step",
    )(*[pltpu.with_memory_space_constraint(x, pltpu.HBM) for x in args])
    results = pl.pallas_call(
        finish_kernel,
        out_shape=[pltpu.HBM(shape, dtype) for shape, dtype in outs],
        in_specs=[in_vmem] * len(outs),
        out_specs=[in_hbm] * len(outs),
        scratch_shapes=[pltpu.SemaphoreType.DMA((len(outs),))],
        name="finish",
    )(*[pltpu.with_memory_space_constraint(x, pltpu.VMEM) for x in results])
    results = [*results[:5], results[5].T, results[6].T]
    return tuple(x[None] for x in results)


def solution(mesh):
    n_row, n_col, n_grp = mesh.shape["row"], mesh.shape["col"], mesh.shape["grp"]
    tiled = P("grp", "row", "col")
    by_row, by_col = P("grp", "row", None), P("grp", "col", None)
    turned_tiles = P("grp", "col", "row")

    def step(grad, *rest):
        sizes = (n_row, n_col, n_grp, math.sqrt(grad.size))
        return jax.shard_map(
            functools.partial(local, sizes=sizes),
            mesh=mesh,
            in_specs=(tiled, tiled, tiled, by_row, by_col, tiled, turned_tiles),
            out_specs=(tiled, tiled, tiled, by_row, by_col, tiled, turned_tiles),
            check_vma=False,
        )(grad, *rest)

    return step
```

```python
import functools
import math

import jax
import jax.numpy as jnp
from jax import lax
from jax.experimental import pallas as pl
from jax.experimental.pallas import tpu as pltpu
from jax.sharding import PartitionSpec as P

NS_STEPS = 3
NS_COEFFS = (3.4445, -4.775, 2.0315)
BETA_FIRST = 0.9
BETA_SECOND = 0.99
STATISTICS_DECAY = 0.95
ADAM_EPS = 1e-08
NORM_EPS = 1e-06
F32 = jnp.float32
BF16 = jnp.bfloat16
MESH = pl.DeviceIdType.MESH
NN = (((1,), (0,)), ((), ()))
NT = (((1,), (1,)), ((), ()))
TN = (((0,), (0,)), ((), ()))


def mm(a, b, dims=NN):
    return lax.dot_general(a, b, dims, preferred_element_type=F32)


def halves(x):
    hi = x.astype(BF16)
    return hi, (x - hi.astype(F32)).astype(BF16)


def mm3(a, b, dims=NN):
    return mm(a[0], b[0], dims) + (mm(a[0], b[1], dims) + mm(a[1], b[0], dims))


def wire_rows(size, count):
    block = size // count
    return size // 256 * block + block * block // 128


def to_wire(rows, out):
    block, size = rows.shape
    for k in range(size // 256):
        out[k * block:(k + 1) * block] = rows[:, k * 128:(k + 1) * 128]
    fold = block * block // 128
    far = rows[:, size // 2:size // 2 + 128]
    lane = lax.broadcasted_iota(jnp.int32, (fold, 128), 1)
    folded = far[:fold]
    for k in range(1, 128 // block):
        folded = jnp.where(lane >= k * block, pltpu.roll(far[k * fold:(k + 1) * fold], k * block, 1), folded)
    out[size // 256 * block:] = folded


def from_wire(wire, size, block):
    fold = block * block // 128
    folded = wire[size // 256 * block:]
    lane = lax.broadcasted_iota(jnp.int32, (fold, 128), 1)
    far = [folded] + [pltpu.roll(folded, 128 - k * block, 1) for k in range(1, 128 // block)]
    wide = [wire[k * block:(k + 1) * block] for k in range(size // 256)]
    wide.append(jnp.concatenate([jnp.where(lane < block, part, 0.0) for part in far], 0))
    if size > 256:
        wide.append(jnp.zeros((block, size // 2 - 128), F32))
    return jnp.concatenate(wide, 1)


def pack_all(square, wires):
    count = wires.shape[0]
    size = square.shape[0]
    block = size // count
    for t in range(count):
        rows = square[t * block:(t + 1) * block, :]
        to_wire(pltpu.roll(rows, (size - t * block) % size, 1), wires.at[t])


def unpack_all(wires, half, square):
    count = wires.shape[0]
    size = square.shape[0]
    block = size // count
    for t in range(count):
        half[t * block:(t + 1) * block, :] = pltpu.roll(from_wire(wires[t], size, block), t * block, 1)
    shift = block.bit_length() - 1
    for i in range(size // 128):
        for j in range(size // 128):
            r = lax.broadcasted_iota(jnp.int32, (128, 128), 0) + i * 128
            c = lax.broadcasted_iota(jnp.int32, (128, 128), 1) + j * 128
            held = (((c >> shift) - (r >> shift)) & (count - 1)) <= count // 2
            here, there = slice(i * 128, (i + 1) * 128), slice(j * 128, (j + 1) * 128)
            square[here, there] = jnp.where(held, half[here, there], half[there, here].T)


def part(k):
    return slice(k * 256, (k + 1) * 256)


def square_part(hi, lo, i, j):
    if i == j:
        cross = mm(hi[part(i), :], lo[part(i), :], NT)
        return mm(hi[part(i), :], hi[part(i), :], NT) + (cross + cross.T)
    return mm3((hi[part(i), :], lo[part(i), :]), (hi[part(j), :], lo[part(j), :]), NT)


def refine(x, x_hi, x_lo, poly, gram_hi, gram_lo):
    count = x.shape[0] // 256
    upper = [(i, j) for i in range(count) for j in range(i, count)]
    for i in range(count):
        x_hi[part(i), :], x_lo[part(i), :] = halves(x[part(i), :])
    yield
    for i, j in upper:
        gram = square_part(x_hi, x_lo, i, j)
        poly[part(i), part(j)] = gram
        gram_hi[part(i), part(j)], gram_lo[part(i), part(j)] = halves(gram)
        if i != j:
            gram_hi[part(j), part(i)], gram_lo[part(j), part(i)] = halves(gram.T)
        yield
    for i, j in upper:
        block = NS_COEFFS[1] * poly[part(i), part(j)] + NS_COEFFS[2] * square_part(gram_hi, gram_lo, i, j)
        poly[part(i), part(j)] = block
        if i != j:
            poly[part(j), part(i)] = block.T
        yield
    for i in range(count):
        product = mm3(halves(poly[part(i), :]), (x_hi[...], x_lo[...]))
        x[part(i), :] = NS_COEFFS[0] * x[part(i), :] + product
        yield


def stages(size):
    count = size // 256
    return 1 + count * (count + 1) + count


def repeated(times, refs):
    for _ in range(times):
        yield from refine(*refs)


def weave(main, n_main, other, n_other):
    done = 0
    for k in range(n_main):
        next(main)
        while done < min(n_other, (k + 1) * n_other // (n_main - 1)):
            next(other)
            done += 1


def step_kernel(
    sizes,
    g_hbm, m_hbm, v_hbm, ql_hbm, qr_hbm, lold_hbm, rold_hbm,
    upd_ref, first_ref, second_ref, newl_ref, newr_ref, lnew_ref, rnew_ref,
    g_ref, m_ref, v_ref, ql_ref, qr_ref, lold_ref, rold_ref,
    lpart, lin, lgather, lhalf, lfull, rpart, rin, rgather, rhalf, rfull,
    sq_out, sq_line, sq_mid, sq_plane, rot, direction, xl, xr,
    l_hi, l_lo, l_poly, lg_hi, lg_lo, r_hi, r_lo, r_poly, rg_hi, rg_lo,
    in_sems, sq_sems, l_sems, r_sems,
):
    n_row, n_col, n_grp, max_norm = sizes
    left, right = g_hbm.shape
    bl, br = left // n_col, right // n_row
    row, col, grp = lax.axis_index("row"), lax.axis_index("col"), lax.axis_index("grp")
    n_plane = n_col * n_grp
    place = col * n_grp + grp

    def row_peer(d):
        return {"row": lax.rem(row + d, n_row)}

    def col_peer(d):
        return {"col": lax.rem(col + d, n_col)}

    def plane_peer(q):
        other = lax.rem(place + q, n_plane)
        return {"col": other // n_grp, "grp": lax.rem(other, n_grp)}

    def remote(src, dst, sems, k, peer):
        return pltpu.make_async_remote_copy(
            src_ref=src, dst_ref=dst, send_sem=sems.at[k], recv_sem=sems.at[k + 1],
            device_id=peer, device_id_type=MESH,
        )

    def wait(ref, sem):
        pltpu.make_async_copy(ref, ref, sem).wait()

    fetched = [
        pltpu.make_async_copy(src, dst, in_sems.at[k])
        for k, (src, dst) in enumerate([
            (g_hbm, g_ref), (ql_hbm, ql_ref), (qr_hbm, qr_ref), (m_hbm, m_ref), (v_hbm, v_ref),
            (lold_hbm, lold_ref), (rold_hbm, rold_ref),
        ])
    ]
    for copy in fetched:
        copy.start()
    barrier = pltpu.get_barrier_semaphore()

    @pl.loop(1, n_row)
    def _(d):
        pl.semaphore_signal(barrier, inc=1, device_id=row_peer(d), device_id_type=MESH)

    @pl.loop(1, n_plane)
    def _(q):
        pl.semaphore_signal(barrier, inc=1, device_id=plane_peer(q), device_id_type=MESH)

    fetched[0].wait()
    g = g_ref[...]
    gf = g.astype(F32)
    sq_out[...] = jnp.full((1, 128), jnp.sum(gf * gf), F32)
    lfull[...] = mm(g, g, NT)
    pack_all(lfull, lpart)
    rfull[...] = mm(g, g, TN)
    pack_all(rfull, rpart)
    pl.semaphore_wait(barrier, n_plane - 1 + n_row - 1)

    @pl.loop(1, n_row)
    def _(d):
        remote(sq_out, sq_line.at[d - 1], sq_sems, 0, row_peer(d)).start()

    @pl.loop(1, n_row)
    def _(d):
        other = lax.rem(row + d, n_row)
        remote(rpart.at[other], rin.at[d - 1], r_sems, 0, {"row": other}).start()

    @pl.loop(1, n_col)
    def _(d):
        other = lax.rem(col + d, n_col)
        remote(lpart.at[other], lin.at[d - 1], l_sems, 0, {"col": other}).start()

    wait(sq_line, sq_sems.at[1])
    sq_mid[...] = sq_out[...] + jnp.sum(sq_line[...], axis=0)

    @pl.loop(1, n_plane)
    def _(q):
        remote(sq_mid, sq_plane.at[q - 1], sq_sems, 2, plane_peer(q)).start()

    for copy in fetched[1:]:
        copy.wait()
    for i in range(left // 256):
        rows = part(i)
        half_turn = mm(ql_ref[:, rows], g, TN).astype(BF16)
        rot[rows, :] = mm(half_turn, qr_ref[...])

    to_wire(pltpu.roll(lold_ref[...], lax.rem(left - col * bl, left), 1), lgather.at[col])
    to_wire(pltpu.roll(rold_ref[...], lax.rem(right - row * br, right), 1), rgather.at[row])

    wait(sq_plane, sq_sems.at[3])
    total_sq = (sq_mid[...] + jnp.sum(sq_plane[...], axis=0))[:, :1]
    clip = jnp.minimum(1.0, max_norm * lax.rsqrt(total_sq + NORM_EPS))
    clip_sq = clip * clip
    coef_left = (1.0 - STATISTICS_DECAY) * (clip_sq / (right * n_col))
    coef_right = (1.0 - STATISTICS_DECAY) * (clip_sq / (left * n_row))

    wait(lin, l_sems.at[1])
    lsum = lpart[col]
    for d in range(n_col - 1):
        lsum = lsum + lin[d]
    lgather[col] = STATISTICS_DECAY * lgather[col] + coef_left * lsum

    @pl.loop(1, n_col)
    def _(d):
        remote(lgather.at[col], lgather.at[col], l_sems, 2, col_peer(d)).start()

    wait(rin, r_sems.at[1])
    rsum = rpart[row]
    for d in range(n_row - 1):
        rsum = rsum + rin[d]
    rgather[row] = STATISTICS_DECAY * rgather[row] + coef_right * rsum

    @pl.loop(1, n_row)
    def _(d):
        remote(rgather.at[row], rgather.at[row], r_sems, 2, row_peer(d)).start()

    inv_scale = 1.0 / math.sqrt(left * right)
    turn_scale = clip * inv_scale
    for i in range(left // 64):
        rows = slice(i * 64, (i + 1) * 64)
        rotated = rot[rows, :] * turn_scale
        first = BETA_FIRST * m_ref[rows, :].astype(F32) + (1.0 - BETA_FIRST) * rotated
        second = BETA_SECOND * v_ref[rows, :].astype(F32) + (1.0 - BETA_SECOND) * rotated * rotated
        first_ref[rows, :] = first.astype(BF16)
        second_ref[rows, :] = second.astype(BF16)
        direction[rows, :] = (first / (jnp.sqrt(second) + ADAM_EPS)).astype(BF16)
    for i in range(left // 256):
        rows = part(i)
        back_half = mm(ql_ref[rows, :], direction[...]).astype(BF16)
        upd_ref[rows, :] = (mm(back_half, qr_ref[...], NT) * inv_scale).astype(BF16)

    def start(stats_ref, basis_ref, x_ref):
        hi, lo = halves(stats_ref[...])
        product = mm(hi, basis_ref[...]) + mm(lo, basis_ref[...])
        x_ref[...] = product * lax.rsqrt(jnp.sum(product * product) + NORM_EPS)

    wait(lgather.at[pl.ds(0, n_col - 1)], l_sems.at[3])
    unpack_all(lgather, lhalf, lfull)
    lnew_ref[...] = lfull[pl.ds(pl.multiple_of(col * bl, bl), bl)]
    left_refs = (xl, l_hi, l_lo, l_poly, lg_hi, lg_lo)
    right_refs = (xr, r_hi, r_lo, r_poly, rg_hi, rg_lo)
    l_stages, r_stages = stages(left), stages(right)
    start(lfull, ql_ref, xl)
    for _ in repeated(1, left_refs):
        pass
    wait(rgather.at[pl.ds(0, n_row - 1)], r_sems.at[3])
    unpack_all(rgather, rhalf, rfull)
    rnew_ref[...] = rfull[pl.ds(pl.multiple_of(row * br, br), br)]
    start(rfull, qr_ref, xr)
    rest = NS_STEPS - 1
    weave(repeated(rest, left_refs), rest * l_stages, repeated(NS_STEPS, right_refs), NS_STEPS * r_stages)

    newl_ref[...] = (xl[...] * math.sqrt(left)).astype(BF16)
    newr_ref[...] = (xr[...] * math.sqrt(right)).astype(BF16)
    wait(sq_line, sq_sems.at[0])
    wait(sq_plane, sq_sems.at[2])
    wait(lin, l_sems.at[0])
    wait(lgather.at[pl.ds(0, n_col - 1)], l_sems.at[2])
    wait(rin, r_sems.at[0])
    wait(rgather.at[pl.ds(0, n_row - 1)], r_sems.at[2])


def finish_kernel(*refs):
    count = (len(refs) - 1) // 2
    copies = [pltpu.make_async_copy(refs[k], refs[count + k], refs[-1].at[k]) for k in range(count)]
    for copy in copies:
        copy.start()
    for copy in copies:
        copy.wait()


def local(grad, exp_avg, exp_avg_sq, left_basis, right_basis, left_stats, right_stats, sizes):
    n_row, n_col, n_grp, _ = sizes
    args = [x[0] for x in (grad, exp_avg, exp_avg_sq, left_basis, right_basis)]
    args += [left_stats[0].T, right_stats[0].T]
    left, right = args[0].shape
    bl, br = left // n_col, right // n_row
    l_wire, r_wire = wire_rows(left, n_col), wire_rows(right, n_row)
    in_hbm = pl.BlockSpec(memory_space=pltpu.HBM)
    in_vmem = pl.BlockSpec(memory_space=pltpu.VMEM)
    outs = [((left, right), BF16)] * 3 + [
        ((left, left), BF16), ((right, right), BF16), ((bl, left), F32), ((br, right), F32)
    ]
    results = pl.pallas_call(
        functools.partial(step_kernel, sizes),
        out_shape=[pltpu.VMEM(shape, dtype) for shape, dtype in outs],
        in_specs=[in_hbm] * len(args),
        out_specs=[in_vmem] * len(outs),
        scratch_shapes=[
            *[pltpu.VMEM(x.shape, x.dtype) for x in args],
            pltpu.VMEM((n_col, l_wire, 128), F32),
            pltpu.VMEM((n_col - 1, l_wire, 128), F32),
            pltpu.VMEM((n_col, l_wire, 128), F32),
            pltpu.VMEM((left, left), F32),
            pltpu.VMEM((left, left), F32),
            pltpu.VMEM((n_row, r_wire, 128), F32),
            pltpu.VMEM((n_row - 1, r_wire, 128), F32),
            pltpu.VMEM((n_row, r_wire, 128), F32),
            pltpu.VMEM((right, right), F32),
            pltpu.VMEM((right, right), F32),
            pltpu.VMEM((1, 128), F32),
            pltpu.VMEM((n_row - 1, 1, 128), F32),
            pltpu.VMEM((1, 128), F32),
            pltpu.VMEM((n_col * n_grp - 1, 1, 128), F32),
            pltpu.VMEM((left, right), F32),
            pltpu.VMEM((left, right), BF16),
            pltpu.VMEM((left, left), F32),
            pltpu.VMEM((right, right), F32),
            *[pltpu.VMEM((size, size), dtype) for size in (left, right) for dtype in (BF16, BF16, F32, BF16, BF16)],
            pltpu.SemaphoreType.DMA((7,)),
            pltpu.SemaphoreType.DMA((4,)),
            pltpu.SemaphoreType.DMA((4,)),
            pltpu.SemaphoreType.DMA((4,)),
        ],
        compiler_params=pltpu.CompilerParams(
            collective_id=0, has_side_effects=True, vmem_limit_bytes=40 * 1024 * 1024
        ),
        name="step",
    )(*[pltpu.with_memory_space_constraint(x, pltpu.HBM) for x in args])
    results = pl.pallas_call(
        finish_kernel,
        out_shape=[pltpu.HBM(shape, dtype) for shape, dtype in outs],
        in_specs=[in_vmem] * len(outs),
        out_specs=[in_hbm] * len(outs),
        scratch_shapes=[pltpu.SemaphoreType.DMA((len(outs),))],
        name="finish",
    )(*[pltpu.with_memory_space_constraint(x, pltpu.VMEM) for x in results])
    results = [*results[:5], results[5].T, results[6].T]
    return tuple(x[None] for x in results)


def solution(mesh):
    n_row, n_col, n_grp = mesh.shape["row"], mesh.shape["col"], mesh.shape["grp"]
    tiled = P("grp", "row", "col")
    by_row, by_col = P("grp", "row", None), P("grp", "col", None)
    turned_tiles = P("grp", "col", "row")

    def step(grad, *rest):
        sizes = (n_row, n_col, n_grp, math.sqrt(grad.size))
        return jax.shard_map(
            functools.partial(local, sizes=sizes),
            mesh=mesh,
            in_specs=(tiled, tiled, tiled, by_row, by_col, tiled, turned_tiles),
            out_specs=(tiled, tiled, tiled, by_row, by_col, tiled, turned_tiles),
            check_vma=False,
        )(grad, *rest)

    return step
```

```python
import functools
import math

import jax
import jax.numpy as jnp
from jax import lax
from jax.experimental import pallas as pl
from jax.experimental.pallas import tpu as pltpu
from jax.sharding import PartitionSpec as P

NS_STEPS = 3
NS_COEFFS = (3.4445, -4.775, 2.0315)
BETA_FIRST = 0.9
BETA_SECOND = 0.99
STATISTICS_DECAY = 0.95
ADAM_EPS = 1e-08
NORM_EPS = 1e-06
F32 = jnp.float32
BF16 = jnp.bfloat16
MESH = pl.DeviceIdType.MESH
NN = (((1,), (0,)), ((), ()))
NT = (((1,), (1,)), ((), ()))
TN = (((0,), (0,)), ((), ()))


def mm(a, b, dims=NN):
    return lax.dot_general(a, b, dims, preferred_element_type=F32)


def halves(x):
    hi = x.astype(BF16)
    return hi, (x - hi.astype(F32)).astype(BF16)


def mm3(a, b, dims=NN):
    return mm(a[0], b[0], dims) + (mm(a[0], b[1], dims) + mm(a[1], b[0], dims))


def farthest_first(count, width):
    def hops(d, n):
        return min(d % n, -d % n)

    return sorted(range(1, count), key=lambda d: -hops(d // width, count // width) - hops(d, width))


def wire_rows(size, count):
    block = size // count
    return size // 256 * block + block * block // 128


def to_wire(rows, out):
    block, size = rows.shape
    for k in range(size // 256):
        out[k * block:(k + 1) * block] = rows[:, k * 128:(k + 1) * 128]
    fold = block * block // 128
    far = rows[:, size // 2:size // 2 + 128]
    lane = lax.broadcasted_iota(jnp.int32, (fold, 128), 1)
    folded = far[:fold]
    for k in range(1, 128 // block):
        folded = jnp.where(lane >= k * block, pltpu.roll(far[k * fold:(k + 1) * fold], k * block, 1), folded)
    out[size // 256 * block:] = folded


def from_wire(wire, size, block):
    fold = block * block // 128
    folded = wire[size // 256 * block:]
    lane = lax.broadcasted_iota(jnp.int32, (fold, 128), 1)
    far = [folded] + [pltpu.roll(folded, 128 - k * block, 1) for k in range(1, 128 // block)]
    wide = [wire[k * block:(k + 1) * block] for k in range(size // 256)]
    wide.append(jnp.concatenate([jnp.where(lane < block, part, 0.0) for part in far], 0))
    if size > 256:
        wide.append(jnp.zeros((block, size // 2 - 128), F32))
    return jnp.concatenate(wide, 1)


def pack_all(square, wires):
    count = wires.shape[0]
    size = square.shape[0]
    block = size // count
    for t in range(count):
        rows = square[t * block:(t + 1) * block, :]
        to_wire(pltpu.roll(rows, (size - t * block) % size, 1), wires.at[t])


def unpack_all(wires, half, square):
    count = wires.shape[0]
    size = square.shape[0]
    block = size // count
    for t in range(count):
        half[t * block:(t + 1) * block, :] = pltpu.roll(from_wire(wires[t], size, block), t * block, 1)
    shift = block.bit_length() - 1
    for i in range(size // 128):
        for j in range(size // 128):
            r = lax.broadcasted_iota(jnp.int32, (128, 128), 0) + i * 128
            c = lax.broadcasted_iota(jnp.int32, (128, 128), 1) + j * 128
            held = (((c >> shift) - (r >> shift)) & (count - 1)) <= count // 2
            here, there = slice(i * 128, (i + 1) * 128), slice(j * 128, (j + 1) * 128)
            square[here, there] = jnp.where(held, half[here, there], half[there, here].T)


def part(k):
    return slice(k * 256, (k + 1) * 256)


def square_part(hi, lo, i, j):
    if i == j:
        cross = mm(hi[part(i), :], lo[part(i), :], NT)
        return mm(hi[part(i), :], hi[part(i), :], NT) + (cross + cross.T)
    return mm3((hi[part(i), :], lo[part(i), :]), (hi[part(j), :], lo[part(j), :]), NT)


def refine(x, x_hi, x_lo, poly, gram_hi, gram_lo):
    count = x.shape[0] // 256
    upper = [(i, j) for i in range(count) for j in range(i, count)]
    for i in range(count):
        x_hi[part(i), :], x_lo[part(i), :] = halves(x[part(i), :])
    yield
    for i, j in upper:
        gram = square_part(x_hi, x_lo, i, j)
        poly[part(i), part(j)] = gram
        gram_hi[part(i), part(j)], gram_lo[part(i), part(j)] = halves(gram)
        if i != j:
            gram_hi[part(j), part(i)], gram_lo[part(j), part(i)] = halves(gram.T)
        yield
    for i, j in upper:
        block = NS_COEFFS[1] * poly[part(i), part(j)] + NS_COEFFS[2] * square_part(gram_hi, gram_lo, i, j)
        poly[part(i), part(j)] = block
        if i != j:
            poly[part(j), part(i)] = block.T
        yield
    for i in range(count):
        product = mm3(halves(poly[part(i), :]), (x_hi[...], x_lo[...]))
        x[part(i), :] = NS_COEFFS[0] * x[part(i), :] + product
        yield


def stages(size):
    count = size // 256
    return 1 + count * (count + 1) + count


def repeated(times, refs):
    for _ in range(times):
        yield from refine(*refs)


def weave(main, n_main, other, n_other):
    done = 0
    for k in range(n_main):
        next(main)
        while done < min(n_other, (k + 1) * n_other // (n_main - 1)):
            next(other)
            done += 1


def step_kernel(
    sizes,
    g_hbm, m_hbm, v_hbm, ql_hbm, qr_hbm, lold_hbm, rold_hbm,
    upd_ref, first_ref, second_ref, newl_ref, newr_ref, lnew_ref, rnew_ref,
    g_ref, m_ref, v_ref, ql_ref, qr_ref, lold_ref, rold_ref,
    lpart, lin, lgather, lhalf, lfull, rpart, rin, rgather, rhalf, rfull,
    sq_out, sq_line, sq_mid, sq_plane, rot, direction, xl, xr,
    l_hi, l_lo, l_poly, lg_hi, lg_lo, r_hi, r_lo, r_poly, rg_hi, rg_lo,
    in_sems, sq_sems, l_sems, r_sems,
):
    n_row, n_col, n_grp, max_norm = sizes
    left, right = g_hbm.shape
    bl, br = left // n_col, right // n_row
    row, col, grp = lax.axis_index("row"), lax.axis_index("col"), lax.axis_index("grp")
    n_plane = n_col * n_grp
    place = col * n_grp + grp

    side = math.isqrt(n_col)
    row_order = farthest_first(n_row, n_row)
    col_order = farthest_first(n_col, side) if side * side == n_col else range(1, n_col)

    def row_peer(d):
        return {"row": lax.rem(row + d, n_row)}

    def col_peer(d):
        return {"col": lax.rem(col + d, n_col)}

    def plane_peer(q):
        other = lax.rem(place + q, n_plane)
        return {"col": other // n_grp, "grp": lax.rem(other, n_grp)}

    def remote(src, dst, sems, k, peer):
        return pltpu.make_async_remote_copy(
            src_ref=src, dst_ref=dst, send_sem=sems.at[k], recv_sem=sems.at[k + 1],
            device_id=peer, device_id_type=MESH,
        )

    def wait(ref, sem):
        pltpu.make_async_copy(ref, ref, sem).wait()

    fetched = [
        pltpu.make_async_copy(src, dst, in_sems.at[k])
        for k, (src, dst) in enumerate([
            (g_hbm, g_ref), (ql_hbm, ql_ref), (qr_hbm, qr_ref), (m_hbm, m_ref), (v_hbm, v_ref),
            (lold_hbm, lold_ref), (rold_hbm, rold_ref),
        ])
    ]
    for copy in fetched:
        copy.start()
    barrier = pltpu.get_barrier_semaphore()

    @pl.loop(1, n_row)
    def _(d):
        pl.semaphore_signal(barrier, inc=1, device_id=row_peer(d), device_id_type=MESH)

    @pl.loop(1, n_plane)
    def _(q):
        pl.semaphore_signal(barrier, inc=1, device_id=plane_peer(q), device_id_type=MESH)

    fetched[0].wait()
    g = g_ref[...]
    gf = g.astype(F32)
    sq_out[...] = jnp.full((1, 128), jnp.sum(gf * gf), F32)
    lfull[...] = mm(g, g, NT)
    pack_all(lfull, lpart)
    rfull[...] = mm(g, g, TN)
    pack_all(rfull, rpart)
    pl.semaphore_wait(barrier, n_plane - 1 + n_row - 1)

    for d in row_order:
        remote(sq_out, sq_line.at[d - 1], sq_sems, 0, row_peer(d)).start()

    for d in row_order:
        other = lax.rem(row + d, n_row)
        remote(rpart.at[other], rin.at[d - 1], r_sems, 0, {"row": other}).start()

    for d in col_order:
        other = lax.rem(col + d, n_col)
        remote(lpart.at[other], lin.at[d - 1], l_sems, 0, {"col": other}).start()

    wait(sq_line, sq_sems.at[1])
    sq_mid[...] = sq_out[...] + jnp.sum(sq_line[...], axis=0)

    @pl.loop(1, n_plane)
    def _(q):
        remote(sq_mid, sq_plane.at[q - 1], sq_sems, 2, plane_peer(q)).start()

    for copy in fetched[1:]:
        copy.wait()
    for i in range(left // 256):
        rows = part(i)
        half_turn = mm(ql_ref[:, rows], g, TN).astype(BF16)
        rot[rows, :] = mm(half_turn, qr_ref[...])

    to_wire(pltpu.roll(lold_ref[...], lax.rem(left - col * bl, left), 1), lgather.at[col])
    to_wire(pltpu.roll(rold_ref[...], lax.rem(right - row * br, right), 1), rgather.at[row])

    wait(sq_plane, sq_sems.at[3])
    total_sq = (sq_mid[...] + jnp.sum(sq_plane[...], axis=0))[:, :1]
    clip = jnp.minimum(1.0, max_norm * lax.rsqrt(total_sq + NORM_EPS))
    clip_sq = clip * clip
    coef_left = (1.0 - STATISTICS_DECAY) * (clip_sq / (right * n_col))
    coef_right = (1.0 - STATISTICS_DECAY) * (clip_sq / (left * n_row))

    wait(lin, l_sems.at[1])
    lsum = lpart[col]
    for d in range(n_col - 1):
        lsum = lsum + lin[d]
    lgather[col] = STATISTICS_DECAY * lgather[col] + coef_left * lsum

    for d in col_order:
        remote(lgather.at[col], lgather.at[col], l_sems, 2, col_peer(d)).start()

    wait(rin, r_sems.at[1])
    rsum = rpart[row]
    for d in range(n_row - 1):
        rsum = rsum + rin[d]
    rgather[row] = STATISTICS_DECAY * rgather[row] + coef_right * rsum

    for d in row_order:
        remote(rgather.at[row], rgather.at[row], r_sems, 2, row_peer(d)).start()

    inv_scale = 1.0 / math.sqrt(left * right)
    turn_scale = clip * inv_scale
    for i in range(left // 64):
        rows = slice(i * 64, (i + 1) * 64)
        rotated = rot[rows, :] * turn_scale
        first = BETA_FIRST * m_ref[rows, :].astype(F32) + (1.0 - BETA_FIRST) * rotated
        second = BETA_SECOND * v_ref[rows, :].astype(F32) + (1.0 - BETA_SECOND) * rotated * rotated
        first_ref[rows, :] = first.astype(BF16)
        second_ref[rows, :] = second.astype(BF16)
        direction[rows, :] = (first / (jnp.sqrt(second) + ADAM_EPS)).astype(BF16)
    for i in range(left // 256):
        rows = part(i)
        back_half = mm(ql_ref[rows, :], direction[...]).astype(BF16)
        upd_ref[rows, :] = (mm(back_half, qr_ref[...], NT) * inv_scale).astype(BF16)

    def start(stats_ref, basis_ref, x_ref):
        hi, lo = halves(stats_ref[...])
        product = mm(hi, basis_ref[...]) + mm(lo, basis_ref[...])
        x_ref[...] = product * lax.rsqrt(jnp.sum(product * product) + NORM_EPS)

    wait(lgather.at[pl.ds(0, n_col - 1)], l_sems.at[3])
    unpack_all(lgather, lhalf, lfull)
    lnew_ref[...] = lfull[pl.ds(pl.multiple_of(col * bl, bl), bl)]
    left_refs = (xl, l_hi, l_lo, l_poly, lg_hi, lg_lo)
    right_refs = (xr, r_hi, r_lo, r_poly, rg_hi, rg_lo)
    l_stages, r_stages = stages(left), stages(right)
    start(lfull, ql_ref, xl)
    for _ in repeated(1, left_refs):
        pass
    wait(rgather.at[pl.ds(0, n_row - 1)], r_sems.at[3])
    unpack_all(rgather, rhalf, rfull)
    rnew_ref[...] = rfull[pl.ds(pl.multiple_of(row * br, br), br)]
    start(rfull, qr_ref, xr)
    rest = NS_STEPS - 1
    weave(repeated(rest, left_refs), rest * l_stages, repeated(NS_STEPS, right_refs), NS_STEPS * r_stages)

    newl_ref[...] = (xl[...] * math.sqrt(left)).astype(BF16)
    newr_ref[...] = (xr[...] * math.sqrt(right)).astype(BF16)
    wait(sq_line, sq_sems.at[0])
    wait(sq_plane, sq_sems.at[2])
    wait(lin, l_sems.at[0])
    wait(lgather.at[pl.ds(0, n_col - 1)], l_sems.at[2])
    wait(rin, r_sems.at[0])
    wait(rgather.at[pl.ds(0, n_row - 1)], r_sems.at[2])


def finish_kernel(*refs):
    count = (len(refs) - 1) // 2
    copies = [pltpu.make_async_copy(refs[k], refs[count + k], refs[-1].at[k]) for k in range(count)]
    for copy in copies:
        copy.start()
    for copy in copies:
        copy.wait()


def local(grad, exp_avg, exp_avg_sq, left_basis, right_basis, left_stats, right_stats, sizes):
    n_row, n_col, n_grp, _ = sizes
    args = [x[0] for x in (grad, exp_avg, exp_avg_sq, left_basis, right_basis)]
    args += [left_stats[0].T, right_stats[0].T]
    left, right = args[0].shape
    bl, br = left // n_col, right // n_row
    l_wire, r_wire = wire_rows(left, n_col), wire_rows(right, n_row)
    in_hbm = pl.BlockSpec(memory_space=pltpu.HBM)
    in_vmem = pl.BlockSpec(memory_space=pltpu.VMEM)
    outs = [((left, right), BF16)] * 3 + [
        ((left, left), BF16), ((right, right), BF16), ((bl, left), F32), ((br, right), F32)
    ]
    results = pl.pallas_call(
        functools.partial(step_kernel, sizes),
        out_shape=[pltpu.VMEM(shape, dtype) for shape, dtype in outs],
        in_specs=[in_hbm] * len(args),
        out_specs=[in_vmem] * len(outs),
        scratch_shapes=[
            *[pltpu.VMEM(x.shape, x.dtype) for x in args],
            pltpu.VMEM((n_col, l_wire, 128), F32),
            pltpu.VMEM((n_col - 1, l_wire, 128), F32),
            pltpu.VMEM((n_col, l_wire, 128), F32),
            pltpu.VMEM((left, left), F32),
            pltpu.VMEM((left, left), F32),
            pltpu.VMEM((n_row, r_wire, 128), F32),
            pltpu.VMEM((n_row - 1, r_wire, 128), F32),
            pltpu.VMEM((n_row, r_wire, 128), F32),
            pltpu.VMEM((right, right), F32),
            pltpu.VMEM((right, right), F32),
            pltpu.VMEM((1, 128), F32),
            pltpu.VMEM((n_row - 1, 1, 128), F32),
            pltpu.VMEM((1, 128), F32),
            pltpu.VMEM((n_col * n_grp - 1, 1, 128), F32),
            pltpu.VMEM((left, right), F32),
            pltpu.VMEM((left, right), BF16),
            pltpu.VMEM((left, left), F32),
            pltpu.VMEM((right, right), F32),
            *[pltpu.VMEM((size, size), dtype) for size in (left, right) for dtype in (BF16, BF16, F32, BF16, BF16)],
            pltpu.SemaphoreType.DMA((7,)),
            pltpu.SemaphoreType.DMA((4,)),
            pltpu.SemaphoreType.DMA((4,)),
            pltpu.SemaphoreType.DMA((4,)),
        ],
        compiler_params=pltpu.CompilerParams(
            collective_id=0, has_side_effects=True, vmem_limit_bytes=40 * 1024 * 1024
        ),
        name="step",
    )(*[pltpu.with_memory_space_constraint(x, pltpu.HBM) for x in args])
    results = pl.pallas_call(
        finish_kernel,
        out_shape=[pltpu.HBM(shape, dtype) for shape, dtype in outs],
        in_specs=[in_vmem] * len(outs),
        out_specs=[in_hbm] * len(outs),
        scratch_shapes=[pltpu.SemaphoreType.DMA((len(outs),))],
        name="finish",
    )(*[pltpu.with_memory_space_constraint(x, pltpu.VMEM) for x in results])
    results = [*results[:5], results[5].T, results[6].T]
    return tuple(x[None] for x in results)


def solution(mesh):
    n_row, n_col, n_grp = mesh.shape["row"], mesh.shape["col"], mesh.shape["grp"]
    tiled = P("grp", "row", "col")
    by_row, by_col = P("grp", "row", None), P("grp", "col", None)
    turned_tiles = P("grp", "col", "row")

    def step(grad, *rest):
        sizes = (n_row, n_col, n_grp, math.sqrt(grad.size))
        return jax.shard_map(
            functools.partial(local, sizes=sizes),
            mesh=mesh,
            in_specs=(tiled, tiled, tiled, by_row, by_col, tiled, turned_tiles),
            out_specs=(tiled, tiled, tiled, by_row, by_col, tiled, turned_tiles),
            check_vma=False,
        )(grad, *rest)

    return step
```

```python
import functools
import math

import jax
import jax.numpy as jnp
from jax import lax
from jax.experimental import pallas as pl
from jax.experimental.pallas import tpu as pltpu
from jax.sharding import PartitionSpec as P

NS_STEPS = 3
NS_COEFFS = (3.4445, -4.775, 2.0315)
BETA_FIRST = 0.9
BETA_SECOND = 0.99
STATISTICS_DECAY = 0.95
ADAM_EPS = 1e-08
NORM_EPS = 1e-06
F32 = jnp.float32
BF16 = jnp.bfloat16
MESH = pl.DeviceIdType.MESH
NN = (((1,), (0,)), ((), ()))
NT = (((1,), (1,)), ((), ()))
TN = (((0,), (0,)), ((), ()))


def mm(a, b, dims=NN):
    return lax.dot_general(a, b, dims, preferred_element_type=F32)


def halves(x):
    hi = x.astype(BF16)
    return hi, (x - hi.astype(F32)).astype(BF16)


def mm3(a, b, dims=NN):
    return mm(a[0], b[0], dims) + (mm(a[0], b[1], dims) + mm(a[1], b[0], dims))


def farthest_first(count, width):
    def hops(d, n):
        return min(d % n, -d % n)

    return sorted(range(1, count), key=lambda d: -hops(d // width, count // width) - hops(d, width))


def wire_rows(size, count):
    block = size // count
    return size // 256 * block + block * block // 128


def to_wire(rows, out):
    block, size = rows.shape
    for k in range(size // 256):
        out[k * block:(k + 1) * block] = rows[:, k * 128:(k + 1) * 128]
    fold = block * block // 128
    far = rows[:, size // 2:size // 2 + 128]
    lane = lax.broadcasted_iota(jnp.int32, (fold, 128), 1)
    folded = far[:fold]
    for k in range(1, 128 // block):
        folded = jnp.where(lane >= k * block, pltpu.roll(far[k * fold:(k + 1) * fold], k * block, 1), folded)
    out[size // 256 * block:] = folded


def from_wire(wire, size, block):
    fold = block * block // 128
    folded = wire[size // 256 * block:]
    lane = lax.broadcasted_iota(jnp.int32, (fold, 128), 1)
    far = [folded] + [pltpu.roll(folded, 128 - k * block, 1) for k in range(1, 128 // block)]
    wide = [wire[k * block:(k + 1) * block] for k in range(size // 256)]
    wide.append(jnp.concatenate([jnp.where(lane < block, part, 0.0) for part in far], 0))
    if size > 256:
        wide.append(jnp.zeros((block, size // 2 - 128), F32))
    return jnp.concatenate(wide, 1)


def pack_all(square, wires):
    count = wires.shape[0]
    size = square.shape[0]
    block = size // count
    for t in range(count):
        rows = square[t * block:(t + 1) * block, :]
        to_wire(pltpu.roll(rows, (size - t * block) % size, 1), wires.at[t])


def unpack_all(wires, half, square, arrived=None):
    count = wires.shape[0]
    size = square.shape[0]
    block = size // count
    for t in range(count):
        if arrived is not None:
            arrived(t)
        half[t * block:(t + 1) * block, :] = pltpu.roll(from_wire(wires[t], size, block), t * block, 1)
    shift = block.bit_length() - 1
    for i in range(size // 128):
        for j in range(size // 128):
            r = lax.broadcasted_iota(jnp.int32, (128, 128), 0) + i * 128
            c = lax.broadcasted_iota(jnp.int32, (128, 128), 1) + j * 128
            held = (((c >> shift) - (r >> shift)) & (count - 1)) <= count // 2
            here, there = slice(i * 128, (i + 1) * 128), slice(j * 128, (j + 1) * 128)
            square[here, there] = jnp.where(held, half[here, there], half[there, here].T)


def part(k):
    return slice(k * 256, (k + 1) * 256)


def square_part(hi, lo, i, j):
    if i == j:
        cross = mm(hi[part(i), :], lo[part(i), :], NT)
        return mm(hi[part(i), :], hi[part(i), :], NT) + (cross + cross.T)
    return mm3((hi[part(i), :], lo[part(i), :]), (hi[part(j), :], lo[part(j), :]), NT)


def refine(x, x_hi, x_lo, poly, gram_hi, gram_lo):
    count = x.shape[0] // 256
    upper = [(i, j) for i in range(count) for j in range(i, count)]
    for i in range(count):
        x_hi[part(i), :], x_lo[part(i), :] = halves(x[part(i), :])
    yield
    for i, j in upper:
        gram = square_part(x_hi, x_lo, i, j)
        poly[part(i), part(j)] = gram
        gram_hi[part(i), part(j)], gram_lo[part(i), part(j)] = halves(gram)
        if i != j:
            gram_hi[part(j), part(i)], gram_lo[part(j), part(i)] = halves(gram.T)
        yield
    for i, j in upper:
        block = NS_COEFFS[1] * poly[part(i), part(j)] + NS_COEFFS[2] * square_part(gram_hi, gram_lo, i, j)
        poly[part(i), part(j)] = block
        if i != j:
            poly[part(j), part(i)] = block.T
        yield
    for i in range(count):
        product = mm3(halves(poly[part(i), :]), (x_hi[...], x_lo[...]))
        x[part(i), :] = NS_COEFFS[0] * x[part(i), :] + product
        yield


def stages(size):
    count = size // 256
    return 1 + count * (count + 1) + count


def repeated(times, refs):
    for _ in range(times):
        yield from refine(*refs)


def weave(main, n_main, other, n_other):
    done = 0
    for k in range(n_main):
        next(main)
        while done < min(n_other, (k + 1) * n_other // (n_main - 1)):
            next(other)
            done += 1


def step_kernel(
    sizes,
    g_hbm, m_hbm, v_hbm, ql_hbm, qr_hbm, lold_hbm, rold_hbm,
    upd_ref, first_ref, second_ref, newl_ref, newr_ref, lnew_ref, rnew_ref,
    g_ref, m_ref, v_ref, ql_ref, qr_ref, lold_ref, rold_ref,
    lpart, lin, lgather, lhalf, lfull, rpart, rin, rgather, rhalf, rfull,
    sq_out, sq_line, sq_mid, sq_plane, rot, direction, xl, xr,
    l_hi, l_lo, l_poly, lg_hi, lg_lo, r_hi, r_lo, r_poly, rg_hi, rg_lo,
    in_sems, sq_sems, l_sems, r_sems, lg_sems,
):
    n_row, n_col, n_grp, max_norm = sizes
    left, right = g_hbm.shape
    bl, br = left // n_col, right // n_row
    row, col, grp = lax.axis_index("row"), lax.axis_index("col"), lax.axis_index("grp")
    n_plane = n_col * n_grp
    place = col * n_grp + grp

    side = math.isqrt(n_col)
    row_order = farthest_first(n_row, n_row)
    col_order = farthest_first(n_col, side) if side * side == n_col else range(1, n_col)

    def row_peer(d):
        return {"row": lax.rem(row + d, n_row)}

    def col_peer(d):
        return {"col": lax.rem(col + d, n_col)}

    def plane_peer(q):
        other = lax.rem(place + q, n_plane)
        return {"col": other // n_grp, "grp": lax.rem(other, n_grp)}

    def remote(src, dst, sems, k, peer):
        return pltpu.make_async_remote_copy(
            src_ref=src, dst_ref=dst, send_sem=sems.at[k], recv_sem=sems.at[k + 1],
            device_id=peer, device_id_type=MESH,
        )

    def wait(ref, sem):
        pltpu.make_async_copy(ref, ref, sem).wait()

    fetched = [
        pltpu.make_async_copy(src, dst, in_sems.at[k])
        for k, (src, dst) in enumerate([
            (g_hbm, g_ref), (ql_hbm, ql_ref), (qr_hbm, qr_ref), (m_hbm, m_ref), (v_hbm, v_ref),
            (lold_hbm, lold_ref), (rold_hbm, rold_ref),
        ])
    ]
    for copy in fetched:
        copy.start()
    barrier = pltpu.get_barrier_semaphore()

    @pl.loop(1, n_row)
    def _(d):
        pl.semaphore_signal(barrier, inc=1, device_id=row_peer(d), device_id_type=MESH)

    @pl.loop(1, n_plane)
    def _(q):
        pl.semaphore_signal(barrier, inc=1, device_id=plane_peer(q), device_id_type=MESH)

    fetched[0].wait()
    g = g_ref[...]
    gf = g.astype(F32)
    sq_out[...] = jnp.full((1, 128), jnp.sum(gf * gf), F32)
    lfull[...] = mm(g, g, NT)
    pack_all(lfull, lpart)
    rfull[...] = mm(g, g, TN)
    pack_all(rfull, rpart)
    pl.semaphore_wait(barrier, n_plane - 1 + n_row - 1)

    for d in row_order:
        remote(sq_out, sq_line.at[d - 1], sq_sems, 0, row_peer(d)).start()

    for d in row_order:
        other = lax.rem(row + d, n_row)
        remote(rpart.at[other], rin.at[d - 1], r_sems, 0, {"row": other}).start()

    for d in col_order:
        other = lax.rem(col + d, n_col)
        remote(lpart.at[other], lin.at[d - 1], l_sems, 0, {"col": other}).start()

    wait(sq_line, sq_sems.at[1])
    sq_mid[...] = sq_out[...] + jnp.sum(sq_line[...], axis=0)

    @pl.loop(1, n_plane)
    def _(q):
        remote(sq_mid, sq_plane.at[q - 1], sq_sems, 2, plane_peer(q)).start()

    for copy in fetched[1:]:
        copy.wait()
    for i in range(left // 256):
        rows = part(i)
        half_turn = mm(ql_ref[:, rows], g, TN).astype(BF16)
        rot[rows, :] = mm(half_turn, qr_ref[...])

    to_wire(pltpu.roll(lold_ref[...], lax.rem(left - col * bl, left), 1), lgather.at[col])
    to_wire(pltpu.roll(rold_ref[...], lax.rem(right - row * br, right), 1), rgather.at[row])

    wait(sq_plane, sq_sems.at[3])
    total_sq = (sq_mid[...] + jnp.sum(sq_plane[...], axis=0))[:, :1]
    clip = jnp.minimum(1.0, max_norm * lax.rsqrt(total_sq + NORM_EPS))
    clip_sq = clip * clip
    coef_left = (1.0 - STATISTICS_DECAY) * (clip_sq / (right * n_col))
    coef_right = (1.0 - STATISTICS_DECAY) * (clip_sq / (left * n_row))

    wait(lin, l_sems.at[1])
    lsum = lpart[col]
    for d in range(n_col - 1):
        lsum = lsum + lin[d]
    lgather[col] = STATISTICS_DECAY * lgather[col] + coef_left * lsum

    for d in col_order:
        pltpu.make_async_remote_copy(
            src_ref=lgather.at[col], dst_ref=lgather.at[col], send_sem=l_sems.at[2], recv_sem=lg_sems.at[col],
            device_id=col_peer(d), device_id_type=MESH,
        ).start()

    wait(rin, r_sems.at[1])
    rsum = rpart[row]
    for d in range(n_row - 1):
        rsum = rsum + rin[d]
    rgather[row] = STATISTICS_DECAY * rgather[row] + coef_right * rsum

    for d in row_order:
        remote(rgather.at[row], rgather.at[row], r_sems, 2, row_peer(d)).start()

    inv_scale = 1.0 / math.sqrt(left * right)
    turn_scale = clip * inv_scale
    for i in range(left // 64):
        rows = slice(i * 64, (i + 1) * 64)
        rotated = rot[rows, :] * turn_scale
        first = BETA_FIRST * m_ref[rows, :].astype(F32) + (1.0 - BETA_FIRST) * rotated
        second = BETA_SECOND * v_ref[rows, :].astype(F32) + (1.0 - BETA_SECOND) * rotated * rotated
        first_ref[rows, :] = first.astype(BF16)
        second_ref[rows, :] = second.astype(BF16)
        direction[rows, :] = (first / (jnp.sqrt(second) + ADAM_EPS)).astype(BF16)
    for i in range(left // 256):
        rows = part(i)
        back_half = mm(ql_ref[rows, :], direction[...]).astype(BF16)
        upd_ref[rows, :] = (mm(back_half, qr_ref[...], NT) * inv_scale).astype(BF16)

    def start(stats_ref, basis_ref, x_ref):
        hi, lo = halves(stats_ref[...])
        product = mm(hi, basis_ref[...]) + mm(lo, basis_ref[...])
        x_ref[...] = product * lax.rsqrt(jnp.sum(product * product) + NORM_EPS)

    def arrived(t):
        @pl.when(t != col)
        def _():
            wait(lgather.at[t], lg_sems.at[t])

    unpack_all(lgather, lhalf, lfull, arrived)
    lnew_ref[...] = lfull[pl.ds(pl.multiple_of(col * bl, bl), bl)]
    left_refs = (xl, l_hi, l_lo, l_poly, lg_hi, lg_lo)
    right_refs = (xr, r_hi, r_lo, r_poly, rg_hi, rg_lo)
    l_stages, r_stages = stages(left), stages(right)
    start(lfull, ql_ref, xl)
    for _ in repeated(1, left_refs):
        pass
    wait(rgather.at[pl.ds(0, n_row - 1)], r_sems.at[3])
    unpack_all(rgather, rhalf, rfull)
    rnew_ref[...] = rfull[pl.ds(pl.multiple_of(row * br, br), br)]
    start(rfull, qr_ref, xr)
    rest = NS_STEPS - 1
    weave(repeated(rest, left_refs), rest * l_stages, repeated(NS_STEPS, right_refs), NS_STEPS * r_stages)

    newl_ref[...] = (xl[...] * math.sqrt(left)).astype(BF16)
    newr_ref[...] = (xr[...] * math.sqrt(right)).astype(BF16)
    wait(sq_line, sq_sems.at[0])
    wait(sq_plane, sq_sems.at[2])
    wait(lin, l_sems.at[0])
    wait(lgather.at[pl.ds(0, n_col - 1)], l_sems.at[2])
    wait(rin, r_sems.at[0])
    wait(rgather.at[pl.ds(0, n_row - 1)], r_sems.at[2])


def finish_kernel(*refs):
    count = (len(refs) - 1) // 2
    copies = [pltpu.make_async_copy(refs[k], refs[count + k], refs[-1].at[k]) for k in range(count)]
    for copy in copies:
        copy.start()
    for copy in copies:
        copy.wait()


def local(grad, exp_avg, exp_avg_sq, left_basis, right_basis, left_stats, right_stats, sizes):
    n_row, n_col, n_grp, _ = sizes
    args = [x[0] for x in (grad, exp_avg, exp_avg_sq, left_basis, right_basis)]
    args += [left_stats[0].T, right_stats[0].T]
    left, right = args[0].shape
    bl, br = left // n_col, right // n_row
    l_wire, r_wire = wire_rows(left, n_col), wire_rows(right, n_row)
    in_hbm = pl.BlockSpec(memory_space=pltpu.HBM)
    in_vmem = pl.BlockSpec(memory_space=pltpu.VMEM)
    outs = [((left, right), BF16)] * 3 + [
        ((left, left), BF16), ((right, right), BF16), ((bl, left), F32), ((br, right), F32)
    ]
    results = pl.pallas_call(
        functools.partial(step_kernel, sizes),
        out_shape=[pltpu.VMEM(shape, dtype) for shape, dtype in outs],
        in_specs=[in_hbm] * len(args),
        out_specs=[in_vmem] * len(outs),
        scratch_shapes=[
            *[pltpu.VMEM(x.shape, x.dtype) for x in args],
            pltpu.VMEM((n_col, l_wire, 128), F32),
            pltpu.VMEM((n_col - 1, l_wire, 128), F32),
            pltpu.VMEM((n_col, l_wire, 128), F32),
            pltpu.VMEM((left, left), F32),
            pltpu.VMEM((left, left), F32),
            pltpu.VMEM((n_row, r_wire, 128), F32),
            pltpu.VMEM((n_row - 1, r_wire, 128), F32),
            pltpu.VMEM((n_row, r_wire, 128), F32),
            pltpu.VMEM((right, right), F32),
            pltpu.VMEM((right, right), F32),
            pltpu.VMEM((1, 128), F32),
            pltpu.VMEM((n_row - 1, 1, 128), F32),
            pltpu.VMEM((1, 128), F32),
            pltpu.VMEM((n_col * n_grp - 1, 1, 128), F32),
            pltpu.VMEM((left, right), F32),
            pltpu.VMEM((left, right), BF16),
            pltpu.VMEM((left, left), F32),
            pltpu.VMEM((right, right), F32),
            *[pltpu.VMEM((size, size), dtype) for size in (left, right) for dtype in (BF16, BF16, F32, BF16, BF16)],
            pltpu.SemaphoreType.DMA((7,)),
            pltpu.SemaphoreType.DMA((4,)),
            pltpu.SemaphoreType.DMA((4,)),
            pltpu.SemaphoreType.DMA((4,)),
            pltpu.SemaphoreType.DMA((n_col,)),
        ],
        compiler_params=pltpu.CompilerParams(
            collective_id=0, has_side_effects=True, vmem_limit_bytes=40 * 1024 * 1024
        ),
        name="step",
    )(*[pltpu.with_memory_space_constraint(x, pltpu.HBM) for x in args])
    results = pl.pallas_call(
        finish_kernel,
        out_shape=[pltpu.HBM(shape, dtype) for shape, dtype in outs],
        in_specs=[in_vmem] * len(outs),
        out_specs=[in_hbm] * len(outs),
        scratch_shapes=[pltpu.SemaphoreType.DMA((len(outs),))],
        name="finish",
    )(*[pltpu.with_memory_space_constraint(x, pltpu.VMEM) for x in results])
    results = [*results[:5], results[5].T, results[6].T]
    return tuple(x[None] for x in results)


def solution(mesh):
    n_row, n_col, n_grp = mesh.shape["row"], mesh.shape["col"], mesh.shape["grp"]
    tiled = P("grp", "row", "col")
    by_row, by_col = P("grp", "row", None), P("grp", "col", None)
    turned_tiles = P("grp", "col", "row")

    def step(grad, *rest):
        sizes = (n_row, n_col, n_grp, math.sqrt(grad.size))
        return jax.shard_map(
            functools.partial(local, sizes=sizes),
            mesh=mesh,
            in_specs=(tiled, tiled, tiled, by_row, by_col, tiled, turned_tiles),
            out_specs=(tiled, tiled, tiled, by_row, by_col, tiled, turned_tiles),
            check_vma=False,
        )(grad, *rest)

    return step
```
